32 devices in a mesh: pipe: 4 (over z), tensor: 4 (over y, x), dp: 2 (over core).
Axes of the slice: x: 2, y: 2, z: 4, core: 2. Of those that a mesh axis runs over, the one named last changes fastest.
Arguments:
- entry_grads: float32 [2, 4, 64, 3584], P(None, 'pipe', ('dp', 'tensor')), may hold values from -6 to 6
- fresh_grads: float32 [2, 2, 64, 3584], P(None, None, ('dp', 'tensor')), may hold values from -6 to 6
- saved_inputs: bfloat16 [2, 3, 4, 64, 3584], P(None, None, 'pipe', 'dp'), may hold values from -6 to 6
- w_in: bfloat16 [2, 4, 3584, 2048], P(None, 'pipe', None, 'tensor'), may hold values from -0.09375 to 0.09375
- w_down: bfloat16 [2, 4, 1024, 3584], P(None, 'pipe', 'tensor'), may hold values from -0.1875 to 0.1875
Outputs:
- hand_offs: float32 [2, 3, 4, 64, 3584], P(None, None, 'pipe', ('dp', 'tensor'))
- grad_w_in: float32 [2, 4, 3584, 2048], P(None, 'pipe', 'dp', 'tensor')
- grad_w_down: float32 [2, 4, 1024, 3584], P(None, 'pipe', 'tensor', 'dp')
The draws below stay inside these ranges and needn't reach their ends.
All inputs are finite; a program needn't handle non-finite values.
Results may differ from the reference program's by a relative error of at most 0.02.
Values may be sent and summed in bfloat16 or wider, within the bound.
No kernel may reach another device: no remote copies, remote signals or barrier semaphores. Data moves between devices by JAX's collectives and lax.ppermute only.
A program may use at most 128 MiB of HBM per device.

```python
import jax
import jax.numpy as jnp
from jax import lax

D = 3584
HID = 1024
K_STEPS = 3
MB_ROWS = 32
SECTIONS = 4
ROWS = 64
HSH = 256
N_TENSOR = 4
N_DP = 2


def level_of(own_key, extent, shards, smallest, top_value):
    def one(dim, blocks):
        draws = jax.random.uniform(jax.random.fold_in(jax.random.fold_in(own_key, 6), dim), (blocks,), jnp.float32, smallest / len(shards), top_value / len(shards))
        return jnp.repeat(jnp.exp(draws), extent[dim] // blocks).reshape((-1,) + (1,) * (len(extent) - dim - 1))

    level = one(*shards[0])
    for cut in shards[1:]:
        level = level * one(*cut)
    return level


def normal_values(key, shape, scale, limit, pieces=(), held_as=jnp.bfloat16):
    result = jax.random.normal(key, shape, jnp.float32) * scale
    if len(pieces) > 0:
        result = level_of(key, shape, pieces, -0.22, 0.18) * result
    return jnp.clip(result, min=-limit, max=limit).astype(held_as)


def setup_inputs(seed: int = 0) -> dict:
    keys = jax.random.split(jax.random.key(seed), 6)
    entry_grads = normal_values(keys[0], (2, SECTIONS, ROWS, D), 1.0, 6.0, ((1, 4), (2, 8)), jnp.float32)
    fresh_grads = normal_values(keys[1], (2, K_STEPS - 1, ROWS, D), 1.0, 6.0, ((2, 8),), jnp.float32)
    saved_inputs = normal_values(keys[2], (2, K_STEPS, SECTIONS, ROWS, D), 1.0, 6.0, ((2, 4), (3, 2)))
    w_in = normal_values(keys[3], (2, SECTIONS, D, 2 * HID), D ** -0.5, 0.09375, ((1, 4), (3, 4)))
    w_down = normal_values(keys[4], (2, SECTIONS, HID, D), HID ** -0.5, 0.1875, ((1, 4), (2, 4)))
    return {"entry_grads": entry_grads, "fresh_grads": fresh_grads, "saved_inputs": saved_inputs, "w_in": w_in, "w_down": w_down}


def block_grads(inputs, incoming, w_in_layer, w_down_layer):
    projected = jnp.dot(inputs, w_in_layer, preferred_element_type=jnp.float32)
    projected = projected.reshape(ROWS, N_TENSOR, 2, HSH)
    gate_part = projected[:, :, 0, :].reshape(ROWS, HID)
    up_part = projected[:, :, 1, :].reshape(ROWS, HID)
    sigmoid_val = jax.nn.sigmoid(gate_part)
    activated = gate_part * sigmoid_val
    hidden = (activated * up_part).astype(jnp.bfloat16)
    dy_rows = incoming.astype(jnp.bfloat16)
    hidden_grad = jnp.dot(dy_rows, w_down_layer.T, preferred_element_type=jnp.float32)
    gate_grad = hidden_grad * up_part * sigmoid_val * (1.0 + gate_part * (1.0 - sigmoid_val))
    up_grad = hidden_grad * activated
    pre_grad = jnp.stack([gate_grad.reshape(ROWS, N_TENSOR, HSH), up_grad.reshape(ROWS, N_TENSOR, HSH)], axis=2)
    pre_grad = pre_grad.reshape(ROWS, 2 * HID).astype(jnp.bfloat16)
    parts = jnp.einsum('rtc,dtc->trd', pre_grad.reshape(ROWS, N_TENSOR, 2 * HSH).astype(jnp.float32),
                       w_in_layer.reshape(D, N_TENSOR, 2 * HSH).astype(jnp.float32))
    rounded = lax.optimization_barrier(parts.astype(jnp.bfloat16)).astype(jnp.float32)
    handed = incoming + jnp.sum(rounded, axis=0)
    in_term = jnp.einsum('nrd,nrc->ndc', inputs.reshape(N_DP, MB_ROWS, D).astype(jnp.float32),
                         pre_grad.reshape(N_DP, MB_ROWS, 2 * HID).astype(jnp.float32))
    down_term = jnp.einsum('nrh,nrd->nhd', hidden.reshape(N_DP, MB_ROWS, HID).astype(jnp.float32),
                           dy_rows.reshape(N_DP, MB_ROWS, D).astype(jnp.float32))
    return handed, in_term, down_term


def replica_total(terms):
    rounded = lax.optimization_barrier(terms.astype(jnp.bfloat16)).astype(jnp.float32)
    return jnp.sum(rounded, axis=0)


def reference(entry_grads, fresh_grads, saved_inputs, w_in, w_down):
    results = {}
    in_grads = {}
    down_grads = {}
    for direction in range(2):
        if direction == 0:
            order = list(range(SECTIONS - 1, -1, -1))
        else:
            order = list(range(SECTIONS))
        for section in order:
            in_accum = jnp.zeros((N_DP, D, 2 * HID), jnp.float32)
            down_accum = jnp.zeros((N_DP, HID, D), jnp.float32)
            for window_step in range(K_STEPS):
                if window_step == 0:
                    incoming = entry_grads[direction, section]
                else:
                    neighbour = section + 1 if direction == 0 else section - 1
                    if 0 <= neighbour < SECTIONS:
                        incoming = results[(direction, window_step - 1, neighbour)]
                    else:
                        incoming = fresh_grads[direction, window_step - 1]
                handed, in_term, down_term = block_grads(saved_inputs[direction, window_step, section], incoming,
                                                         w_in[direction, section], w_down[direction, section])
                results[(direction, window_step, section)] = handed
                in_accum = in_accum + in_term
                down_accum = down_accum + down_term
            in_grads[(direction, section)] = replica_total(in_accum)
            down_grads[(direction, section)] = replica_total(down_accum)
    hand_offs = jnp.stack([jnp.stack([jnp.stack([results[(direction, window_step, section)] for section in range(SECTIONS)])
                                      for window_step in range(K_STEPS)]) for direction in range(2)])
    grad_w_in = jnp.stack([jnp.stack([in_grads[(direction, section)] for section in range(SECTIONS)]) for direction in range(2)])
    grad_w_down = jnp.stack([jnp.stack([down_grads[(direction, section)] for section in range(SECTIONS)]) for direction in range(2)])
    return hand_offs, grad_w_in, grad_w_down
```

```python
import jax
import jax.numpy as jnp
from jax import lax
from jax.sharding import PartitionSpec as P

AXES = ("pipe", "tensor", "dp")
BF16 = jnp.bfloat16
F32 = jnp.float32


def ring_pairs(sections, tensor_count, replicas, shift):
    pairs = []
    for p in range(sections):
        for t in range(tensor_count):
            to = (t + shift) % tensor_count
            for q in range(replicas):
                step = 1 if q % 2 else -1
                if 0 <= p + step < sections:
                    target = ((p + step) * tensor_count + to) * replicas + q
                else:
                    target = (p * tensor_count + to) * replicas + (q ^ 1)
                pairs.append(((p * tensor_count + t) * replicas + q, target))
    return pairs


def local(entry_grads, fresh_grads, saved_inputs, w_in, w_down):
    section = lax.axis_index("pipe")
    sections = lax.axis_size("pipe")
    place = lax.axis_index("tensor")
    tensor_count = lax.axis_size("tensor")
    replica = lax.axis_index("dp")
    replicas = lax.axis_size("dp")
    core = lax.rem(replica, 2)
    steps, _, batch_rows, width = saved_inputs.shape[1:]
    shard_rows = batch_rows // tensor_count
    hidden_width = w_down.shape[2]
    part_width = width // replicas

    def mine(x):
        return lax.dynamic_index_in_dim(x, core, 0, keepdims=False)

    def theirs(x):
        return lax.dynamic_index_in_dim(x, 1 - core, 0, keepdims=False)

    def to_core(x, offset=1):
        return lax.ppermute(x, "dp", [(i, i ^ offset) for i in range(replicas)])

    def rotate(x, shift):
        return lax.ppermute(x, "tensor", [(i, (i + shift) % tensor_count) for i in range(tensor_count)])

    entry = entry_grads[:, 0]
    entry_other = to_core(theirs(entry).astype(BF16))
    payload = jnp.concatenate([mine(entry).astype(BF16), entry_other])
    blocks = [payload] + [rotate(payload, s) for s in range(1, tensor_count)]
    incoming = jnp.concatenate([mine(entry), entry_other.astype(F32)])

    fresh_own = theirs(fresh_grads).astype(BF16)
    fresh_other = to_core(mine(fresh_grads).astype(BF16))
    fresh_pair = jnp.concatenate([fresh_other, fresh_own], axis=1)
    at_end = section == jnp.where(core == 0, 0, sections - 1)

    saved = saved_inputs[:, :, 0]
    saved_own = mine(saved)
    saved_other = to_core(theirs(saved))
    ordered = []
    for s in range(tensor_count):
        start = lax.rem(place - s + tensor_count, tensor_count) * shard_rows
        ordered.append(lax.dynamic_slice_in_dim(saved_own, start, shard_rows, axis=1))
        ordered.append(lax.dynamic_slice_in_dim(saved_other, start, shard_rows, axis=1))
    rows = jnp.concatenate(ordered, axis=1)

    w_in_dir = mine(w_in[:, 0])
    w_down_dir = mine(w_down[:, 0])
    projected = jnp.einsum("krd,dc->krc", rows, w_in_dir, preferred_element_type=F32)
    gate = projected[:, :, :hidden_width]
    up = projected[:, :, hidden_width:]
    sigmoid_val = jax.nn.sigmoid(gate)
    activated = gate * sigmoid_val
    hidden = (activated * up).astype(BF16)
    gate_factor = up * sigmoid_val * (1.0 + gate * (1.0 - sigmoid_val))

    block_rows = 2 * shard_rows
    own_hand, other_hand, all_dy, all_pre = [], [], [], []
    for k in range(steps):
        dy = jnp.concatenate(blocks)
        dh = jnp.einsum("rd,hd->rh", dy, w_down_dir, preferred_element_type=F32)
        pre_grad = jnp.concatenate([dh * gate_factor[k], dh * activated[k]], axis=1).astype(BF16)
        part = jnp.einsum("rc,dc->rd", pre_grad, w_in_dir, preferred_element_type=F32).astype(BF16)
        summed = part[:block_rows].astype(F32)
        for s in range(1, tensor_count):
            summed = summed + rotate(part[s * block_rows:(s + 1) * block_rows], -s).astype(F32)
        handed = incoming + summed
        if k + 1 < steps:
            payload = jnp.where(at_end, fresh_pair[k], handed.astype(BF16))
            blocks = [lax.ppermute(payload, AXES, ring_pairs(sections, tensor_count, replicas, s))
                      for s in range(tensor_count)]
        own_hand.append(handed[:shard_rows])
        if k == 0:
            other_hand.append(theirs(entry) + to_core(summed[shard_rows:]))
        else:
            other_hand.append(to_core(handed[shard_rows:]))
        incoming = blocks[0].astype(F32)
        all_dy.append(dy)
        all_pre.append(pre_grad)
    dy_rows = jnp.stack(all_dy)
    pre_rows = jnp.stack(all_pre)

    def columns(x, owner):
        return lax.dynamic_slice_in_dim(x, owner * part_width, part_width, axis=2)

    in_terms = [0.0, 0.0]
    down_terms = [0.0, 0.0]
    for offset in range(replicas):
        owner = jnp.bitwise_xor(replica, offset)
        pieces = [columns(rows, owner), pre_rows, hidden, columns(dy_rows, owner)]
        if offset:
            pieces = [to_core(x, offset) for x in pieces]
        rows_part, pre_part, hidden_part, dy_part = pieces
        which = offset % 2
        in_terms[which] = in_terms[which] + jnp.einsum("krd,krc->dc", rows_part, pre_part, preferred_element_type=F32)
        down_terms[which] = down_terms[which] + jnp.einsum("krh,krd->hd", hidden_part, dy_part, preferred_element_type=F32)

    def by_direction(own, other):
        return jnp.where(core == 0, jnp.stack([own, other]), jnp.stack([other, own]))

    hand_offs = by_direction(jnp.stack(own_hand), jnp.stack(other_hand))[:, :, None]
    grad_w_in = by_direction(*in_terms)[:, None]
    grad_w_down = by_direction(*down_terms)[:, None]
    return (hand_offs, grad_w_in, grad_w_down)


def solution(mesh):
    placed = (
        P(None, "pipe", ("dp", "tensor"), None),
        P(None, None, ("dp", "tensor"), None),
        P(None, None, "pipe", "dp", None),
        P(None, "pipe", None, "tensor"),
        P(None, "pipe", "tensor", None),
    )
    return jax.shard_map(
        local,
        mesh=mesh,
        in_specs=placed,
        out_specs=(
            P(None, None, "pipe", ("dp", "tensor"), None),
            P(None, "pipe", "dp", "tensor"),
            P(None, "pipe", "tensor", "dp"),
        ),
        check_vma=False,
    )
```

```python
import functools

import jax
import jax.numpy as jnp
from jax import lax
from jax.experimental import pallas as pl
from jax.experimental.pallas import tpu as pltpu
from jax.sharding import PartitionSpec as P

AXES = ("pipe", "tensor", "dp")
BF16 = jnp.bfloat16
F32 = jnp.float32


def ring_pairs(sections, tensor_count, replicas, shift):
    pairs = []
    for p in range(sections):
        for t in range(tensor_count):
            to = (t + shift) % tensor_count
            for q in range(replicas):
                step = 1 if q % 2 else -1
                if 0 <= p + step < sections:
                    target = ((p + step) * tensor_count + to) * replicas + q
                else:
                    target = (p * tensor_count + to) * replicas + (q ^ 1)
                pairs.append(((p * tensor_count + t) * replicas + q, target))
    return pairs


def lane_block(width, most):
    best = 128
    for size in range(128, most + 1, 128):
        if width % size == 0:
            best = size
    return best


def factors_kernel(places, _, own_ref, peer_ref, w_ref, payload_ref, gate_ref, up_ref, hidden_ref, total, mixed):
    steps, batch_rows, depth = own_ref.shape[1], own_ref.shape[3], own_ref.shape[4]
    shard_rows = batch_rows // places
    hidden_width = hidden_ref.shape[2]
    count = steps * batch_rows
    step = pl.program_id(0)
    rows = jnp.concatenate(
        [own_ref[...].reshape(count, depth), peer_ref[...].reshape(count, depth)], axis=0
    )
    product = jnp.dot(rows, w_ref[0, 0], preferred_element_type=F32)

    @pl.when(step == 0)
    def _():
        total[...] = product

    @pl.when(step > 0)
    def _():
        total[...] += product

    @pl.when(step == pl.num_programs(0) - 1)
    def _():
        for k in range(steps):
            for j in range(places):
                for r in range(2):
                    source = (r * steps + k) * batch_rows + j * shard_rows
                    target = (2 * j + r) * shard_rows
                    mixed[k, target:target + shard_rows] = total[source:source + shard_rows]
        gate = mixed[:, :, :hidden_width]
        up = mixed[:, :, hidden_width:]
        sigmoid_val = jax.nn.sigmoid(gate)
        activated = gate * sigmoid_val
        gate_ref[...] = up * sigmoid_val * (1.0 + gate * (1.0 - sigmoid_val))
        up_ref[...] = activated
        hidden_ref[...] = (activated * up).astype(BF16)


def weight_grads_kernel(steps, replicas, places, _, *refs):
    saved = refs[:replicas]
    pre = refs[replicas:replicas + replicas * steps]
    hidden = refs[replicas + replicas * steps:2 * replicas + replicas * steps]
    dy = refs[2 * replicas + replicas * steps:2 * replicas + 2 * replicas * steps]
    in_ref, down_ref, pre_rows, hidden_rows = refs[-4:]
    batch_rows, block = saved[0].shape[3], saved[0].shape[4]
    pair_rows = 2 * batch_rows
    shard_rows = batch_rows // places
    count = steps * batch_rows

    def columns_of(parity):
        return jnp.concatenate(
            [dy[offset * steps + k][...] for offset in range(parity, replicas, 2) for k in range(steps)], axis=0
        )

    for parity in range(2):

        @pl.when(pl.program_id(0) == parity)
        def _(parity=parity):
            @pl.when(pl.program_id(1) == 0)
            def _():
                for pair in range(replicas // 2):
                    offset = 2 * pair + parity
                    hidden_rows[pair * 2 * count:(pair + 1) * 2 * count] = hidden[offset][...].reshape(
                        2 * count, hidden[offset].shape[2]
                    )
                    for k in range(steps):
                        values = pre[offset * steps + k][...].astype(F32)
                        for r in range(2):
                            half = jnp.concatenate(
                                [
                                    values[(2 * j + r) * shard_rows:(2 * j + r + 1) * shard_rows]
                                    for j in range(places)
                                ],
                                axis=0,
                            )
                            start = ((2 * pair + (r ^ parity)) * steps + k) * batch_rows
                            pre_rows[start:start + batch_rows] = half.astype(BF16)

            down_ref[0, 0] = lax.dot_general(
                hidden_rows[...], columns_of(parity), (((0,), (0,)), ((), ())), preferred_element_type=F32
            )

    inputs = jnp.concatenate([x[...].reshape(count, block) for x in saved], axis=0)
    in_ref[0, 0] = lax.dot_general(
        inputs, pre_rows[...], (((0,), (0,)), ((), ())), preferred_element_type=F32
    )


def local(entry_grads, fresh_grads, saved_inputs, w_in, w_down):
    section = lax.axis_index("pipe")
    sections = lax.axis_size("pipe")
    place = lax.axis_index("tensor")
    tensor_count = lax.axis_size("tensor")
    replica = lax.axis_index("dp")
    replicas = lax.axis_size("dp")
    core = lax.rem(replica, 2)
    steps, _, batch_rows, width = saved_inputs.shape[1:]
    shard_rows = batch_rows // tensor_count
    block_rows = 2 * shard_rows
    pair_rows = 2 * batch_rows
    hidden_width = w_down.shape[2]
    part_width = width // replicas

    def mine(x):
        return jnp.where(core == 0, x[0], x[1])

    def theirs(x):
        return jnp.where(core == 0, x[1], x[0])

    def indexed(x):
        return lax.dynamic_index_in_dim(x, core, 0, keepdims=False)

    def by_direction(own, other):
        return jnp.where(core == 0, jnp.stack([own, other]), jnp.stack([other, own]))

    def to_core(x, offset=1):
        return lax.ppermute(x, "dp", [(i, i ^ offset) for i in range(replicas)])

    def rotate(x, shift):
        return lax.ppermute(x, "tensor", [(i, (i + shift) % tensor_count) for i in range(tensor_count)])

    def placed(blocks):
        rows = []
        for source in range(tensor_count):
            shift = lax.rem(place - source + tensor_count, tensor_count)
            block = blocks[0]
            for i in range(1, tensor_count):
                block = jnp.where(shift == i, blocks[i], block)
            rows.append(block)
        return jnp.concatenate(rows)

    entry = entry_grads[:, 0]
    entry_peer = to_core(entry_grads)[:, 0]
    incoming = jnp.concatenate([mine(entry), mine(entry_peer)])
    payload = incoming.astype(BF16)
    blocks = [payload] + [rotate(payload, s) for s in range(1, tensor_count)]
    saved = [saved_inputs] + [to_core(saved_inputs, offset) for offset in range(1, replicas)]
    which = jnp.stack([core, replica]).astype(jnp.int32)
    depth = lane_block(width, 512)
    gate_factor, activated, hidden = pl.pallas_call(
        functools.partial(factors_kernel, tensor_count),
        grid_spec=pltpu.PrefetchScalarGridSpec(
            num_scalar_prefetch=1,
            grid=(width // depth,),
            in_specs=[
                pl.BlockSpec((1, steps, 1, batch_rows, depth), lambda i, at: (at[0], 0, 0, 0, i)),
                pl.BlockSpec((1, steps, 1, batch_rows, depth), lambda i, at: (at[0], 0, 0, 0, i)),
                pl.BlockSpec((1, 1, depth, 2 * hidden_width), lambda i, at: (at[0], 0, i, 0)),
                pl.BlockSpec(memory_space=pl.ANY),
            ],
            out_specs=[pl.BlockSpec((steps, pair_rows, hidden_width), lambda i, at: (0, 0, 0))] * 3,
            scratch_shapes=[
                pltpu.VMEM((2 * steps * batch_rows, 2 * hidden_width), F32),
                pltpu.VMEM((steps, pair_rows, 2 * hidden_width), F32),
            ],
        ),
        out_shape=[
            jax.ShapeDtypeStruct((steps, pair_rows, hidden_width), F32),
            jax.ShapeDtypeStruct((steps, pair_rows, hidden_width), F32),
            jax.ShapeDtypeStruct((steps, pair_rows, hidden_width), BF16),
        ],
        compiler_params=pltpu.CompilerParams(vmem_limit_bytes=16 << 20),
        cost_estimate=pl.CostEstimate(flops=0, bytes_accessed=0, transcendentals=0),
        name="factors",
    )(which, saved[0], saved[1], w_in, payload)

    fresh_pair = jnp.concatenate(
        [to_core(mine(fresh_grads).astype(BF16)), theirs(fresh_grads).astype(BF16)], axis=1
    )
    at_end = section == jnp.where(core == 0, 0, sections - 1)
    w_in_dir = indexed(w_in[:, 0])
    w_down_dir = indexed(w_down[:, 0])

    blocks, gate_factor, activated = lax.optimization_barrier((blocks, gate_factor, activated))

    def weight_grads():
        hidden_all = [to_core(hidden, o) if o else hidden for o in range(replicas)]
        block = lane_block(part_width, 1024)
        blocks_each = part_width // block
        return pl.pallas_call(
            functools.partial(weight_grads_kernel, steps, replicas, tensor_count),
            grid_spec=pltpu.PrefetchScalarGridSpec(
                num_scalar_prefetch=1,
                grid=(2, blocks_each),
                in_specs=[
                    pl.BlockSpec(
                        (1, steps, 1, batch_rows, block),
                        lambda i, j, at: (at[0] ^ i, 0, 0, 0, at[1] * blocks_each + j),
                    )
                ] * replicas
                + [pl.BlockSpec((pair_rows, 2 * hidden_width), lambda i, j, at: (0, 0))] * (replicas * steps)
                + [pl.BlockSpec((steps, pair_rows, hidden_width), lambda i, j, at: (0, 0, 0))] * replicas
                + [pl.BlockSpec((pair_rows, block), lambda i, j, at: (0, at[1] * blocks_each + j))] * (replicas * steps),
                out_specs=[
                    pl.BlockSpec((1, 1, block, 2 * hidden_width), lambda i, j, at: (at[0] ^ i, 0, j, 0)),
                    pl.BlockSpec((1, 1, hidden_width, block), lambda i, j, at: (at[0] ^ i, 0, 0, j)),
                ],
                scratch_shapes=[
                    pltpu.VMEM((replicas * steps * batch_rows, 2 * hidden_width), BF16),
                    pltpu.VMEM((replicas * steps * batch_rows, hidden_width), BF16),
                ],
            ),
            out_shape=[
                jax.ShapeDtypeStruct((2, 1, part_width, 2 * hidden_width), F32),
                jax.ShapeDtypeStruct((2, 1, hidden_width, part_width), F32),
            ],
            compiler_params=pltpu.CompilerParams(vmem_limit_bytes=24 << 20),
            cost_estimate=pl.CostEstimate(flops=0, bytes_accessed=0, transcendentals=0),
            name="weight_grads",
        )(
            which,
            *saved,
            *[pre_all[k][o] for o in range(replicas) for k in range(steps)],
            *hidden_all,
            *[dy_all[k][o] for o in range(replicas) for k in range(steps)],
        )

    hand_offs = jnp.zeros((2, steps, shard_rows, width), F32)
    dy_all, pre_all = [], []
    for k in range(steps):
        dy = placed(blocks)
        dh = jnp.einsum("rd,hd->rh", dy, w_down_dir, preferred_element_type=F32)
        pre_grad = jnp.concatenate([dh * gate_factor[k], dh * activated[k]], axis=1).astype(BF16)
        part = jnp.einsum("rc,dc->rd", pre_grad, w_in_dir, preferred_element_type=F32).astype(BF16)
        part = part.reshape(tensor_count, block_rows, width)

        def part_for(target):
            return lax.dynamic_index_in_dim(part, target, 0, keepdims=False)

        own_part = part_for(place)
        parts = []
        for s in range(1, tensor_count):
            parts.append(rotate(part_for(lax.rem(place + s, tensor_count)), s))
        dy_all.append([to_core(dy, o) if o else dy for o in range(replicas)])
        pre_all.append([to_core(pre_grad, o) if o else pre_grad for o in range(replicas)])
        if k + 1 == steps:
            parts, grads = lax.optimization_barrier((parts, weight_grads()))
        summed = own_part.astype(F32)
        for x in parts:
            summed = summed + x.astype(F32)
        handed = incoming + summed
        if k + 1 < steps:
            payload = jnp.where(at_end, fresh_pair[k], handed.astype(BF16))
            blocks = [
                lax.ppermute(payload, AXES, ring_pairs(sections, tensor_count, replicas, s))
                for s in range(tensor_count)
            ]
        if k == 0:
            other = theirs(entry) + to_core(summed[shard_rows:])
        else:
            other = to_core(handed[shard_rows:])
        hand_offs = hand_offs.at[:, k].set(by_direction(handed[:shard_rows], other))
        incoming = blocks[0].astype(F32)
    return (hand_offs[:, :, None], *grads)


def solution(mesh):
    placed = (
        P(None, "pipe", ("dp", "tensor"), None),
        P(None, None, ("dp", "tensor"), None),
        P(None, None, "pipe", "dp", None),
        P(None, "pipe", None, "tensor"),
        P(None, "pipe", "tensor", None),
    )
    return jax.shard_map(
        local,
        mesh=mesh,
        in_specs=placed,
        out_specs=(
            P(None, None, "pipe", ("dp", "tensor"), None),
            P(None, "pipe", "dp", "tensor"),
            P(None, "pipe", "tensor", "dp"),
        ),
        check_vma=False,
    )
```

```python
import functools

import jax
import jax.numpy as jnp
from jax import lax
from jax.experimental import pallas as pl
from jax.experimental.pallas import tpu as pltpu
from jax.sharding import PartitionSpec as P

AXES = ("pipe", "tensor", "dp")
BF16 = jnp.bfloat16
F32 = jnp.float32


def ring_pairs(sections, tensor_count, replicas, shift):
    pairs = []
    for p in range(sections):
        for t in range(tensor_count):
            to = (t + shift) % tensor_count
            for q in range(replicas):
                step = 1 if q % 2 else -1
                if 0 <= p + step < sections:
                    target = ((p + step) * tensor_count + to) * replicas + q
                else:
                    target = (p * tensor_count + to) * replicas + (q ^ 1)
                pairs.append(((p * tensor_count + t) * replicas + q, target))
    return pairs


def lane_block(width, most):
    best = 128
    for size in range(128, most + 1, 128):
        if width % size == 0:
            best = size
    return best


def factors_kernel(
    places, at, own_ref, peer_ref, w_ref, down_ref, fresh_ref, _,
    gate_ref, up_ref, hidden_ref, send_ref, keep_ref, w_copy, down_copy, total, mixed
):
    steps, batch_rows, depth = own_ref.shape[1], own_ref.shape[3], own_ref.shape[4]
    shard_rows = batch_rows // places
    hidden_width = hidden_ref.shape[2]
    count = steps * batch_rows
    step = pl.program_id(0)
    rows = jnp.concatenate(
        [own_ref[...].reshape(count, depth), peer_ref[...].reshape(count, depth)], axis=0
    )
    weights = w_ref[0, 0]
    product = jnp.dot(rows, weights, preferred_element_type=F32)
    w_copy[...] = weights
    down_copy[...] = down_ref[0, 0]

    @pl.when(step == 0)
    def _():
        total[...] = product
        send_ref[...] = fresh_ref[at[0]].astype(BF16)
        keep_ref[...] = fresh_ref[1 - at[0]].astype(BF16)

    @pl.when(step > 0)
    def _():
        total[...] += product

    @pl.when(step == pl.num_programs(0) - 1)
    def _():
        for k in range(steps):
            for j in range(places):
                for r in range(2):
                    source = (r * steps + k) * batch_rows + j * shard_rows
                    target = (2 * j + r) * shard_rows
                    mixed[k, target:target + shard_rows] = total[source:source + shard_rows]
        gate = mixed[:, :, :hidden_width]
        up = mixed[:, :, hidden_width:]
        sigmoid_val = jax.nn.sigmoid(gate)
        activated = gate * sigmoid_val
        gate_ref[...] = up * sigmoid_val * (1.0 + gate * (1.0 - sigmoid_val))
        up_ref[...] = activated
        hidden_ref[...] = (activated * up).astype(BF16)


def weight_grads_kernel(steps, replicas, places, _, *refs):
    saved = refs[:replicas]
    pre = refs[replicas:replicas + replicas * steps]
    hidden = refs[replicas + replicas * steps:2 * replicas + replicas * steps]
    dy = refs[2 * replicas + replicas * steps:2 * replicas + 2 * replicas * steps]
    in_ref, down_ref, pre_rows, hidden_rows = refs[-4:]
    batch_rows, block = saved[0].shape[3], saved[0].shape[4]
    pair_rows = 2 * batch_rows
    shard_rows = batch_rows // places
    count = steps * batch_rows

    def columns_of(parity):
        return jnp.concatenate(
            [dy[offset * steps + k][...] for offset in range(parity, replicas, 2) for k in range(steps)], axis=0
        )

    for parity in range(2):

        @pl.when(pl.program_id(0) == parity)
        def _(parity=parity):
            @pl.when(pl.program_id(1) == 0)
            def _():
                for pair in range(replicas // 2):
                    offset = 2 * pair + parity
                    hidden_rows[pair * 2 * count:(pair + 1) * 2 * count] = hidden[offset][...].reshape(
                        2 * count, hidden[offset].shape[2]
                    )
                    for k in range(steps):
                        values = pre[offset * steps + k][...].astype(F32)
                        for r in range(2):
                            half = jnp.concatenate(
                                [
                                    values[(2 * j + r) * shard_rows:(2 * j + r + 1) * shard_rows]
                                    for j in range(places)
                                ],
                                axis=0,
                            )
                            start = ((2 * pair + (r ^ parity)) * steps + k) * batch_rows
                            pre_rows[start:start + batch_rows] = half.astype(BF16)

            down_ref[0, 0] = lax.dot_general(
                hidden_rows[...], columns_of(parity), (((0,), (0,)), ((), ())), preferred_element_type=F32
            )

    inputs = jnp.concatenate([x[...].reshape(count, block) for x in saved], axis=0)
    in_ref[0, 0] = lax.dot_general(
        inputs, pre_rows[...], (((0,), (0,)), ((), ())), preferred_element_type=F32
    )


def local(entry_grads, fresh_grads, saved_inputs, w_in, w_down):
    section = lax.axis_index("pipe")
    sections = lax.axis_size("pipe")
    place = lax.axis_index("tensor")
    tensor_count = lax.axis_size("tensor")
    replica = lax.axis_index("dp")
    replicas = lax.axis_size("dp")
    core = lax.rem(replica, 2)
    steps, _, batch_rows, width = saved_inputs.shape[1:]
    shard_rows = batch_rows // tensor_count
    block_rows = 2 * shard_rows
    pair_rows = 2 * batch_rows
    hidden_width = w_down.shape[2]
    part_width = width // replicas

    def mine(x):
        return jnp.where(core == 0, x[0], x[1])

    def theirs(x):
        return jnp.where(core == 0, x[1], x[0])

    def indexed(x):
        return lax.dynamic_index_in_dim(x, core, 0, keepdims=False)

    def by_direction(own, other):
        return jnp.where(core == 0, jnp.stack([own, other]), jnp.stack([other, own]))

    def to_core(x, offset=1):
        return lax.ppermute(x, "dp", [(i, i ^ offset) for i in range(replicas)])

    def rotate(x, shift):
        return lax.ppermute(x, "tensor", [(i, (i + shift) % tensor_count) for i in range(tensor_count)])

    def placed(blocks):
        rows = []
        for source in range(tensor_count):
            shift = lax.rem(place - source + tensor_count, tensor_count)
            block = blocks[0]
            for i in range(1, tensor_count):
                block = jnp.where(shift == i, blocks[i], block)
            rows.append(block)
        return jnp.concatenate(rows)

    entry = entry_grads[:, 0]
    entry_peer = to_core(entry_grads)[:, 0]
    incoming = jnp.concatenate([mine(entry), mine(entry_peer)])
    payload = incoming.astype(BF16)
    blocks = [payload] + [rotate(payload, s) for s in range(1, tensor_count)]
    saved = [saved_inputs] + [to_core(saved_inputs, offset) for offset in range(1, replicas)]
    which = jnp.stack([core, replica]).astype(jnp.int32)
    depth = lane_block(width, 1792)
    gate_factor, activated, hidden, fresh_send, fresh_keep, w_in_dir, w_down_dir = pl.pallas_call(
        functools.partial(factors_kernel, tensor_count),
        grid_spec=pltpu.PrefetchScalarGridSpec(
            num_scalar_prefetch=1,
            grid=(width // depth,),
            in_specs=[
                pl.BlockSpec((1, steps, 1, batch_rows, depth), lambda i, at: (at[0], 0, 0, 0, i)),
                pl.BlockSpec((1, steps, 1, batch_rows, depth), lambda i, at: (at[0], 0, 0, 0, i)),
                pl.BlockSpec((1, 1, depth, 2 * hidden_width), lambda i, at: (at[0], 0, i, 0)),
                pl.BlockSpec((1, 1, hidden_width, depth), lambda i, at: (at[0], 0, 0, i)),
                pl.BlockSpec(fresh_grads.shape, lambda i, at: (0, 0, 0, 0)),
                pl.BlockSpec(memory_space=pl.ANY),
            ],
            out_specs=[pl.BlockSpec((steps, pair_rows, hidden_width), lambda i, at: (0, 0, 0))] * 3
            + [pl.BlockSpec(fresh_grads.shape[1:], lambda i, at: (0, 0, 0))] * 2
            + [
                pl.BlockSpec((depth, 2 * hidden_width), lambda i, at: (i, 0)),
                pl.BlockSpec((hidden_width, depth), lambda i, at: (0, i)),
            ],
            scratch_shapes=[
                pltpu.VMEM((2 * steps * batch_rows, 2 * hidden_width), F32),
                pltpu.VMEM((steps, pair_rows, 2 * hidden_width), F32),
            ],
        ),
        out_shape=[
            jax.ShapeDtypeStruct((steps, pair_rows, hidden_width), F32),
            jax.ShapeDtypeStruct((steps, pair_rows, hidden_width), F32),
            jax.ShapeDtypeStruct((steps, pair_rows, hidden_width), BF16),
        ]
        + [jax.ShapeDtypeStruct(fresh_grads.shape[1:], BF16)] * 2
        + [
            jax.ShapeDtypeStruct((width, 2 * hidden_width), BF16),
            jax.ShapeDtypeStruct((hidden_width, width), BF16),
        ],
        compiler_params=pltpu.CompilerParams(vmem_limit_bytes=16 << 20),
        cost_estimate=pl.CostEstimate(flops=0, bytes_accessed=0, transcendentals=0),
        name="factors",
    )(
        which,
        pltpu.with_memory_space_constraint(saved[0], pltpu.HBM),
        saved[1],
        pltpu.with_memory_space_constraint(w_in, pltpu.HBM),
        pltpu.with_memory_space_constraint(w_down, pltpu.HBM),
        fresh_grads,
        payload,
    )

    fresh_pair = jnp.concatenate([to_core(fresh_send), fresh_keep], axis=1)
    at_end = section == jnp.where(core == 0, 0, sections - 1)

    blocks, gate_factor, activated = lax.optimization_barrier((blocks, gate_factor, activated))

    def weight_grads():
        hidden_all = [to_core(hidden, o) if o else hidden for o in range(replicas)]
        block = lane_block(part_width, 1024)
        blocks_each = part_width // block
        return pl.pallas_call(
            functools.partial(weight_grads_kernel, steps, replicas, tensor_count),
            grid_spec=pltpu.PrefetchScalarGridSpec(
                num_scalar_prefetch=1,
                grid=(2, blocks_each),
                in_specs=[
                    pl.BlockSpec(
                        (1, steps, 1, batch_rows, block),
                        lambda i, j, at: (at[0] ^ i, 0, 0, 0, at[1] * blocks_each + j),
                    )
                ] * replicas
                + [pl.BlockSpec((pair_rows, 2 * hidden_width), lambda i, j, at: (0, 0))] * (replicas * steps)
                + [pl.BlockSpec((steps, pair_rows, hidden_width), lambda i, j, at: (0, 0, 0))] * replicas
                + [pl.BlockSpec((pair_rows, block), lambda i, j, at: (0, at[1] * blocks_each + j))] * (replicas * steps),
                out_specs=[
                    pl.BlockSpec((1, 1, block, 2 * hidden_width), lambda i, j, at: (at[0] ^ i, 0, j, 0)),
                    pl.BlockSpec((1, 1, hidden_width, block), lambda i, j, at: (at[0] ^ i, 0, 0, j)),
                ],
                scratch_shapes=[
                    pltpu.VMEM((replicas * steps * batch_rows, 2 * hidden_width), BF16),
                    pltpu.VMEM((replicas * steps * batch_rows, hidden_width), BF16),
                ],
            ),
            out_shape=[
                jax.ShapeDtypeStruct((2, 1, part_width, 2 * hidden_width), F32),
                jax.ShapeDtypeStruct((2, 1, hidden_width, part_width), F32),
            ],
            compiler_params=pltpu.CompilerParams(vmem_limit_bytes=24 << 20),
            cost_estimate=pl.CostEstimate(flops=0, bytes_accessed=0, transcendentals=0),
            name="weight_grads",
        )(
            which,
            *saved,
            *[pre_all[k][o] for o in range(replicas) for k in range(steps)],
            *hidden_all,
            *[dy_all[k][o] for o in range(replicas) for k in range(steps)],
        )

    hand_offs = jnp.zeros((2, steps, shard_rows, width), F32)
    dy_all, pre_all = [], []
    for k in range(steps):
        dy = placed(blocks)
        dh = jnp.einsum("rd,hd->rh", dy, w_down_dir, preferred_element_type=F32)
        pre_grad = jnp.concatenate([dh * gate_factor[k], dh * activated[k]], axis=1).astype(BF16)
        part = jnp.einsum("rc,dc->rd", pre_grad, w_in_dir, preferred_element_type=F32).astype(BF16)
        part = part.reshape(tensor_count, block_rows, width)

        def part_for(target):
            return lax.dynamic_index_in_dim(part, target, 0, keepdims=False)

        own_part = part_for(place)
        parts = []
        for s in range(1, tensor_count):
            parts.append(rotate(part_for(lax.rem(place + s, tensor_count)), s))
        dy_all.append([to_core(dy, o) if o else dy for o in range(replicas)])
        pre_all.append([to_core(pre_grad, o) if o else pre_grad for o in range(replicas)])
        if k + 1 == steps:
            parts, grads = lax.optimization_barrier((parts, weight_grads()))
        summed = own_part.astype(F32)
        for x in parts:
            summed = summed + x.astype(F32)
        handed = incoming + summed
        if k + 1 < steps:
            payload = jnp.where(at_end, fresh_pair[k], handed.astype(BF16))
            blocks = [
                lax.ppermute(payload, AXES, ring_pairs(sections, tensor_count, replicas, s))
                for s in range(tensor_count)
            ]
        if k == 0:
            other = theirs(entry) + to_core(summed[shard_rows:])
        else:
            other = to_core(handed[shard_rows:])
        hand_offs = hand_offs.at[:, k].set(by_direction(handed[:shard_rows], other))
        incoming = blocks[0].astype(F32)
    return (hand_offs[:, :, None], *grads)


def solution(mesh):
    placed = (
        P(None, "pipe", ("dp", "tensor"), None),
        P(None, None, ("dp", "tensor"), None),
        P(None, None, "pipe", "dp", None),
        P(None, "pipe", None, "tensor"),
        P(None, "pipe", "tensor", None),
    )
    return jax.shard_map(
        local,
        mesh=mesh,
        in_specs=placed,
        out_specs=(
            P(None, None, "pipe", ("dp", "tensor"), None),
            P(None, "pipe", "dp", "tensor"),
            P(None, "pipe", "tensor", "dp"),
        ),
        check_vma=False,
    )
```

```python
import functools

import jax
import jax.numpy as jnp
from jax import lax
from jax.experimental import pallas as pl
from jax.experimental.pallas import tpu as pltpu
from jax.sharding import PartitionSpec as P

AXES = ("pipe", "tensor", "dp")
BF16 = jnp.bfloat16
F32 = jnp.float32


def ring_pairs(sections, tensor_count, replicas, shift):
    pairs = []
    for p in range(sections):
        for t in range(tensor_count):
            to = (t + shift) % tensor_count
            for q in range(replicas):
                step = 1 if q % 2 else -1
                if 0 <= p + step < sections:
                    target = ((p + step) * tensor_count + to) * replicas + q
                else:
                    target = (p * tensor_count + to) * replicas + (q ^ 1)
                pairs.append(((p * tensor_count + t) * replicas + q, target))
    return pairs


def lane_block(width, most):
    best = 128
    for size in range(128, most + 1, 128):
        if width % size == 0:
            best = size
    return best


def factors_kernel(
    places, at, own_ref, peer_ref, w_ref, down_ref, fresh_ref, _,
    gate_ref, up_ref, hidden_ref, send_ref, keep_ref, w_copy, down_copy, total, mixed
):
    steps, batch_rows, depth = own_ref.shape[1], own_ref.shape[3], own_ref.shape[4]
    shard_rows = batch_rows // places
    hidden_width = hidden_ref.shape[2]
    count = steps * batch_rows
    step = pl.program_id(0)
    rows = jnp.concatenate(
        [own_ref[...].reshape(count, depth), peer_ref[...].reshape(count, depth)], axis=0
    )
    weights = w_ref[0, 0]
    product = jnp.dot(rows, weights, preferred_element_type=F32)
    w_copy[...] = weights.T
    down_copy[...] = down_ref[0, 0].T

    @pl.when(step == 0)
    def _():
        total[...] = product
        send_ref[...] = fresh_ref[at[0]].astype(BF16)
        keep_ref[...] = fresh_ref[1 - at[0]].astype(BF16)

    @pl.when(step > 0)
    def _():
        total[...] += product

    @pl.when(step == pl.num_programs(0) - 1)
    def _():
        for k in range(steps):
            for j in range(places):
                for r in range(2):
                    source = (r * steps + k) * batch_rows + j * shard_rows
                    target = (2 * j + r) * shard_rows
                    mixed[k, target:target + shard_rows] = total[source:source + shard_rows]
        gate = mixed[:, :, :hidden_width]
        up = mixed[:, :, hidden_width:]
        sigmoid_val = jax.nn.sigmoid(gate)
        activated = gate * sigmoid_val
        gate_ref[...] = up * sigmoid_val * (1.0 + gate * (1.0 - sigmoid_val))
        up_ref[...] = activated
        hidden_ref[...] = (activated * up).astype(BF16)


def weight_grads_kernel(steps, replicas, places, _, *refs):
    saved = refs[:replicas]
    pre = refs[replicas:replicas + replicas * steps]
    hidden = refs[replicas + replicas * steps:2 * replicas + replicas * steps]
    dy = refs[2 * replicas + replicas * steps:2 * replicas + 2 * replicas * steps]
    in_ref, down_ref, pre_rows, hidden_rows = refs[-4:]
    batch_rows, block = saved[0].shape[3], saved[0].shape[4]
    pair_rows = 2 * batch_rows
    shard_rows = batch_rows // places
    count = steps * batch_rows

    def columns_of(parity):
        return jnp.concatenate(
            [dy[offset * steps + k][...] for offset in range(parity, replicas, 2) for k in range(steps)], axis=0
        )

    for parity in range(2):

        @pl.when(pl.program_id(0) == parity)
        def _(parity=parity):
            @pl.when(pl.program_id(1) == 0)
            def _():
                for pair in range(replicas // 2):
                    offset = 2 * pair + parity
                    hidden_rows[pair * 2 * count:(pair + 1) * 2 * count] = hidden[offset][...].reshape(
                        2 * count, hidden[offset].shape[2]
                    )
                    for k in range(steps):
                        values = pre[offset * steps + k][...].astype(F32)
                        for r in range(2):
                            half = jnp.concatenate(
                                [
                                    values[(2 * j + r) * shard_rows:(2 * j + r + 1) * shard_rows]
                                    for j in range(places)
                                ],
                                axis=0,
                            )
                            start = ((2 * pair + (r ^ parity)) * steps + k) * batch_rows
                            pre_rows[start:start + batch_rows] = half.astype(BF16)

            down_ref[0, 0] = lax.dot_general(
                hidden_rows[...], columns_of(parity), (((0,), (0,)), ((), ())), preferred_element_type=F32
            )

    inputs = jnp.concatenate([x[...].reshape(count, block) for x in saved], axis=0)
    in_ref[0, 0] = lax.dot_general(
        inputs, pre_rows[...], (((0,), (0,)), ((), ())), preferred_element_type=F32
    )


def local(entry_grads, fresh_grads, saved_inputs, w_in, w_down):
    section = lax.axis_index("pipe")
    sections = lax.axis_size("pipe")
    place = lax.axis_index("tensor")
    tensor_count = lax.axis_size("tensor")
    replica = lax.axis_index("dp")
    replicas = lax.axis_size("dp")
    core = lax.rem(replica, 2)
    steps, _, batch_rows, width = saved_inputs.shape[1:]
    shard_rows = batch_rows // tensor_count
    block_rows = 2 * shard_rows
    pair_rows = 2 * batch_rows
    hidden_width = w_down.shape[2]
    part_width = width // replicas

    def mine(x):
        return jnp.where(core == 0, x[0], x[1])

    def theirs(x):
        return jnp.where(core == 0, x[1], x[0])

    def indexed(x):
        return lax.dynamic_index_in_dim(x, core, 0, keepdims=False)

    def by_direction(own, other):
        return jnp.where(core == 0, jnp.stack([own, other]), jnp.stack([other, own]))

    def to_core(x, offset=1):
        return lax.ppermute(x, "dp", [(i, i ^ offset) for i in range(replicas)])

    def rotate(x, shift):
        return lax.ppermute(x, "tensor", [(i, (i + shift) % tensor_count) for i in range(tensor_count)])

    def placed(blocks):
        rows = []
        for source in range(tensor_count):
            shift = lax.rem(place - source + tensor_count, tensor_count)
            block = blocks[0]
            for i in range(1, tensor_count):
                block = jnp.where(shift == i, blocks[i], block)
            rows.append(block)
        return jnp.concatenate(rows)

    entry = entry_grads[:, 0]
    entry_peer = to_core(entry_grads)[:, 0]
    incoming = jnp.concatenate([mine(entry), mine(entry_peer)])
    payload = incoming.astype(BF16)
    blocks = [payload] + [rotate(payload, s) for s in range(1, tensor_count)]
    saved = [saved_inputs] + [to_core(saved_inputs, offset) for offset in range(1, replicas)]
    which = jnp.stack([core, replica]).astype(jnp.int32)
    depth = lane_block(width, 1792)
    gate_factor, activated, hidden, fresh_send, fresh_keep, w_in_dir, w_down_dir = pl.pallas_call(
        functools.partial(factors_kernel, tensor_count),
        grid_spec=pltpu.PrefetchScalarGridSpec(
            num_scalar_prefetch=1,
            grid=(width // depth,),
            in_specs=[
                pl.BlockSpec((1, steps, 1, batch_rows, depth), lambda i, at: (at[0], 0, 0, 0, i)),
                pl.BlockSpec((1, steps, 1, batch_rows, depth), lambda i, at: (at[0], 0, 0, 0, i)),
                pl.BlockSpec((1, 1, depth, 2 * hidden_width), lambda i, at: (at[0], 0, i, 0)),
                pl.BlockSpec((1, 1, hidden_width, depth), lambda i, at: (at[0], 0, 0, i)),
                pl.BlockSpec(fresh_grads.shape, lambda i, at: (0, 0, 0, 0)),
                pl.BlockSpec(memory_space=pl.ANY),
            ],
            out_specs=[pl.BlockSpec((steps, pair_rows, hidden_width), lambda i, at: (0, 0, 0))] * 3
            + [pl.BlockSpec(fresh_grads.shape[1:], lambda i, at: (0, 0, 0))] * 2
            + [
                pl.BlockSpec((2 * hidden_width, depth), lambda i, at: (0, i)),
                pl.BlockSpec((depth, hidden_width), lambda i, at: (i, 0)),
            ],
            scratch_shapes=[
                pltpu.VMEM((2 * steps * batch_rows, 2 * hidden_width), F32),
                pltpu.VMEM((steps, pair_rows, 2 * hidden_width), F32),
            ],
        ),
        out_shape=[
            jax.ShapeDtypeStruct((steps, pair_rows, hidden_width), F32),
            jax.ShapeDtypeStruct((steps, pair_rows, hidden_width), F32),
            jax.ShapeDtypeStruct((steps, pair_rows, hidden_width), BF16),
        ]
        + [jax.ShapeDtypeStruct(fresh_grads.shape[1:], BF16)] * 2
        + [
            jax.ShapeDtypeStruct((2 * hidden_width, width), BF16),
            jax.ShapeDtypeStruct((width, hidden_width), BF16),
        ],
        compiler_params=pltpu.CompilerParams(vmem_limit_bytes=16 << 20),
        cost_estimate=pl.CostEstimate(flops=0, bytes_accessed=0, transcendentals=0),
        name="factors",
    )(
        which,
        pltpu.with_memory_space_constraint(saved[0], pltpu.HBM),
        saved[1],
        pltpu.with_memory_space_constraint(w_in, pltpu.HBM),
        pltpu.with_memory_space_constraint(w_down, pltpu.HBM),
        pltpu.with_memory_space_constraint(fresh_grads, pltpu.HBM),
        payload,
    )

    fresh_pair = jnp.concatenate([to_core(fresh_send), fresh_keep], axis=1)
    at_end = section == jnp.where(core == 0, 0, sections - 1)

    blocks, gate_factor, activated = lax.optimization_barrier((blocks, gate_factor, activated))

    def weight_grads():
        hidden_all = [to_core(hidden, o) if o else hidden for o in range(replicas)]
        block = lane_block(part_width, 1024)
        blocks_each = part_width // block
        return pl.pallas_call(
            functools.partial(weight_grads_kernel, steps, replicas, tensor_count),
            grid_spec=pltpu.PrefetchScalarGridSpec(
                num_scalar_prefetch=1,
                grid=(2, blocks_each),
                in_specs=[
                    pl.BlockSpec(
                        (1, steps, 1, batch_rows, block),
                        lambda i, j, at: (at[0] ^ i, 0, 0, 0, at[1] * blocks_each + j),
                    )
                ] * replicas
                + [pl.BlockSpec((pair_rows, 2 * hidden_width), lambda i, j, at: (0, 0))] * (replicas * steps)
                + [pl.BlockSpec((steps, pair_rows, hidden_width), lambda i, j, at: (0, 0, 0))] * replicas
                + [pl.BlockSpec((pair_rows, block), lambda i, j, at: (0, at[1] * blocks_each + j))] * (replicas * steps),
                out_specs=[
                    pl.BlockSpec((1, 1, block, 2 * hidden_width), lambda i, j, at: (at[0] ^ i, 0, j, 0)),
                    pl.BlockSpec((1, 1, hidden_width, block), lambda i, j, at: (at[0] ^ i, 0, 0, j)),
                ],
                scratch_shapes=[
                    pltpu.VMEM((replicas * steps * batch_rows, 2 * hidden_width), BF16),
                    pltpu.VMEM((replicas * steps * batch_rows, hidden_width), BF16),
                ],
            ),
            out_shape=[
                jax.ShapeDtypeStruct((2, 1, part_width, 2 * hidden_width), F32),
                jax.ShapeDtypeStruct((2, 1, hidden_width, part_width), F32),
            ],
            compiler_params=pltpu.CompilerParams(vmem_limit_bytes=24 << 20),
            cost_estimate=pl.CostEstimate(flops=0, bytes_accessed=0, transcendentals=0),
            name="weight_grads",
        )(
            which,
            *saved,
            *[pre_all[k][o] for o in range(replicas) for k in range(steps)],
            *hidden_all,
            *[dy_all[k][o] for o in range(replicas) for k in range(steps)],
        )

    hand_offs = jnp.zeros((2, steps, shard_rows, width), F32)
    dy_all, pre_all = [], []
    for k in range(steps):
        dy = placed(blocks)
        dh = jnp.einsum("rd,dh->rh", dy, w_down_dir, preferred_element_type=F32)
        pre_grad = jnp.concatenate([dh * gate_factor[k], dh * activated[k]], axis=1).astype(BF16)
        part = jnp.einsum("rc,cd->rd", pre_grad, w_in_dir, preferred_element_type=F32).astype(BF16)
        dy_all.append([to_core(dy, o) if o else dy for o in range(replicas)])
        if k + 1 == steps:
            part, dy_all[k] = lax.optimization_barrier((part, dy_all[k]))
        part = part.reshape(tensor_count, block_rows, width)

        def part_for(target):
            return lax.dynamic_index_in_dim(part, target, 0, keepdims=False)

        own_part = part_for(place)
        parts = []
        for s in range(1, tensor_count):
            parts.append(rotate(part_for(lax.rem(place + s, tensor_count)), s))
        pre_all.append([to_core(pre_grad, o) if o else pre_grad for o in range(replicas)])
        if k + 1 == steps:
            parts, grads = lax.optimization_barrier((parts, weight_grads()))
        summed = own_part.astype(F32)
        for x in parts:
            summed = summed + x.astype(F32)
        handed = incoming + summed
        if k + 1 < steps:
            payload = jnp.where(at_end, fresh_pair[k], handed.astype(BF16))
            blocks = [
                lax.ppermute(payload, AXES, ring_pairs(sections, tensor_count, replicas, s))
                for s in range(tensor_count)
            ]
        if k == 0:
            other = theirs(entry) + to_core(summed[shard_rows:])
        else:
            other = to_core(handed[shard_rows:])
        if 0 < k < steps - 1:
            blocks, other = lax.optimization_barrier((blocks, other))
        hand_offs = hand_offs.at[:, k].set(by_direction(handed[:shard_rows], other))
        incoming = blocks[0].astype(F32)
    return (hand_offs[:, :, None], *grads)


def solution(mesh):
    placed = (
        P(None, "pipe", ("dp", "tensor"), None),
        P(None, None, ("dp", "tensor"), None),
        P(None, None, "pipe", "dp", None),
        P(None, "pipe", None, "tensor"),
        P(None, "pipe", "tensor", None),
    )
    return jax.shard_map(
        local,
        mesh=mesh,
        in_specs=placed,
        out_specs=(
            P(None, None, "pipe", ("dp", "tensor"), None),
            P(None, "pipe", "dp", "tensor"),
            P(None, "pipe", "tensor", "dp"),
        ),
        check_vma=False,
    )
```

```python
import functools

import jax
import jax.numpy as jnp
from jax import lax
from jax.experimental import pallas as pl
from jax.experimental.pallas import tpu as pltpu
from jax.sharding import PartitionSpec as P

AXES = ("pipe", "tensor", "dp")
BF16 = jnp.bfloat16
F32 = jnp.float32


def ring_pairs(sections, tensor_count, replicas, shift):
    pairs = []
    for p in range(sections):
        for t in range(tensor_count):
            to = (t + shift) % tensor_count
            for q in range(replicas):
                step = 1 if q % 2 else -1
                if 0 <= p + step < sections:
                    target = ((p + step) * tensor_count + to) * replicas + q
                else:
                    target = (p * tensor_count + to) * replicas + (q ^ 1)
                pairs.append(((p * tensor_count + t) * replicas + q, target))
    return pairs


def lane_block(width, most):
    best = 128
    for size in range(128, most + 1, 128):
        if width % size == 0:
            best = size
    return best


def factors_kernel(
    places, at, own_ref, peer_ref, w_ref, down_ref, fresh_ref, fresh_peer_ref, _,
    gate_ref, up_ref, hidden_ref, fresh_out, w_copy, down_copy, total, mixed
):
    steps, batch_rows, depth = own_ref.shape[1], own_ref.shape[3], own_ref.shape[4]
    shard_rows = batch_rows // places
    hidden_width = hidden_ref.shape[2]
    count = steps * batch_rows
    step = pl.program_id(0)
    rows = jnp.concatenate(
        [own_ref[...].reshape(count, depth), peer_ref[...].reshape(count, depth)], axis=0
    )
    weights = w_ref[0, 0]
    product = jnp.dot(rows, weights, preferred_element_type=F32)
    w_copy[...] = weights.T
    down_copy[...] = down_ref[0, 0].T

    @pl.when(step == 0)
    def _():
        total[...] = product
        for k in range(fresh_out.shape[0]):
            fresh_out[k] = jnp.concatenate(
                [fresh_peer_ref[1 - at[0], k], fresh_ref[1 - at[0], k]], axis=0
            ).astype(BF16)

    @pl.when(step > 0)
    def _():
        total[...] += product

    @pl.when(step == pl.num_programs(0) - 1)
    def _():
        for k in range(steps):
            for j in range(places):
                for r in range(2):
                    source = (r * steps + k) * batch_rows + j * shard_rows
                    target = (2 * j + r) * shard_rows
                    mixed[k, target:target + shard_rows] = total[source:source + shard_rows]
        gate = mixed[:, :, :hidden_width]
        up = mixed[:, :, hidden_width:]
        sigmoid_val = jax.nn.sigmoid(gate)
        activated = gate * sigmoid_val
        gate_ref[...] = up * sigmoid_val * (1.0 + gate * (1.0 - sigmoid_val))
        up_ref[...] = activated
        hidden_ref[...] = (activated * up).astype(BF16)


def weight_grads_kernel(steps, replicas, places, _, *refs):
    saved, pre, dy = refs[:replicas], refs[replicas:2 * replicas], refs[2 * replicas:3 * replicas]
    in_ref, down_ref, pre_rows, hidden_rows = refs[-4:]
    batch_rows, block = saved[0].shape[3], saved[0].shape[4]
    shard_rows = batch_rows // places
    hidden_width = hidden_rows.shape[1]
    count = steps * batch_rows

    for parity in range(2):

        @pl.when(pl.program_id(0) == parity)
        def _(parity=parity):
            @pl.when(pl.program_id(1) == 0)
            def _():
                for pair in range(replicas // 2):
                    held = pre[2 * pair + parity]
                    hidden_rows[pair * 2 * count:(pair + 1) * 2 * count] = held[:, :, 2 * hidden_width:].reshape(
                        2 * count, hidden_width
                    )
                    for k in range(steps):
                        values = held[k, :, :2 * hidden_width].astype(F32)
                        for r in range(2):
                            half = jnp.concatenate(
                                [
                                    values[(2 * j + r) * shard_rows:(2 * j + r + 1) * shard_rows]
                                    for j in range(places)
                                ],
                                axis=0,
                            )
                            start = ((2 * pair + (r ^ parity)) * steps + k) * batch_rows
                            pre_rows[start:start + batch_rows] = half.astype(BF16)

            down_ref[0, 0] = lax.dot_general(
                hidden_rows[...],
                jnp.concatenate([dy[offset][...] for offset in range(parity, replicas, 2)], axis=0),
                (((0,), (0,)), ((), ())),
                preferred_element_type=F32,
            )

    inputs = jnp.concatenate([x[...].reshape(count, block) for x in saved], axis=0)
    in_ref[0, 0] = lax.dot_general(
        inputs, pre_rows[...], (((0,), (0,)), ((), ())), preferred_element_type=F32
    )


def local(entry_grads, fresh_grads, saved_inputs, w_in, w_down):
    section = lax.axis_index("pipe")
    sections = lax.axis_size("pipe")
    place = lax.axis_index("tensor")
    tensor_count = lax.axis_size("tensor")
    replica = lax.axis_index("dp")
    replicas = lax.axis_size("dp")
    core = lax.rem(replica, 2)
    steps, _, batch_rows, width = saved_inputs.shape[1:]
    shard_rows = batch_rows // tensor_count
    block_rows = 2 * shard_rows
    pair_rows = 2 * batch_rows
    hidden_width = w_down.shape[2]
    part_width = width // replicas

    def mine(x):
        return jnp.where(core == 0, x[0], x[1])

    def theirs(x):
        return jnp.where(core == 0, x[1], x[0])

    def indexed(x):
        return lax.dynamic_index_in_dim(x, core, 0, keepdims=False)

    def by_direction(own, other):
        return jnp.where(core == 0, jnp.stack([own, other]), jnp.stack([other, own]))

    def to_core(x, offset=1):
        return lax.ppermute(x, "dp", [(i, i ^ offset) for i in range(replicas)])

    def rotate(x, shift):
        return lax.ppermute(x, "tensor", [(i, (i + shift) % tensor_count) for i in range(tensor_count)])

    def placed(blocks):
        rows = []
        for source in range(tensor_count):
            shift = lax.rem(place - source + tensor_count, tensor_count)
            block = blocks[0]
            for i in range(1, tensor_count):
                block = jnp.where(shift == i, blocks[i], block)
            rows.append(block)
        return jnp.concatenate(rows)

    entry = entry_grads[:, 0]
    entry_peer = to_core(entry_grads)[:, 0]
    fresh_peer = to_core(fresh_grads)
    incoming = jnp.concatenate([mine(entry), mine(entry_peer)])
    payload = incoming.astype(BF16)
    blocks = [payload] + [rotate(payload, s) for s in range(1, tensor_count)]
    saved = [saved_inputs] + [to_core(saved_inputs, offset) for offset in range(1, replicas)]
    which = jnp.stack([core, replica]).astype(jnp.int32)
    depth = lane_block(width, 1792)
    gate_factor, activated, hidden, fresh_pair, w_in_dir, w_down_dir = pl.pallas_call(
        functools.partial(factors_kernel, tensor_count),
        grid_spec=pltpu.PrefetchScalarGridSpec(
            num_scalar_prefetch=1,
            grid=(width // depth,),
            in_specs=[
                pl.BlockSpec((1, steps, 1, batch_rows, depth), lambda i, at: (at[0], 0, 0, 0, i)),
                pl.BlockSpec((1, steps, 1, batch_rows, depth), lambda i, at: (at[0], 0, 0, 0, i)),
                pl.BlockSpec((1, 1, depth, 2 * hidden_width), lambda i, at: (at[0], 0, i, 0)),
                pl.BlockSpec((1, 1, hidden_width, depth), lambda i, at: (at[0], 0, 0, i)),
                pl.BlockSpec(fresh_grads.shape, lambda i, at: (0, 0, 0, 0)),
                pl.BlockSpec(fresh_grads.shape, lambda i, at: (0, 0, 0, 0)),
                pl.BlockSpec(memory_space=pl.ANY),
            ],
            out_specs=[pl.BlockSpec((steps, pair_rows, hidden_width), lambda i, at: (0, 0, 0))] * 3
            + [pl.BlockSpec((steps - 1, block_rows, width), lambda i, at: (0, 0, 0))]
            + [
                pl.BlockSpec((2 * hidden_width, depth), lambda i, at: (0, i)),
                pl.BlockSpec((depth, hidden_width), lambda i, at: (i, 0)),
            ],
            scratch_shapes=[
                pltpu.VMEM((2 * steps * batch_rows, 2 * hidden_width), F32),
                pltpu.VMEM((steps, pair_rows, 2 * hidden_width), F32),
            ],
        ),
        out_shape=[
            jax.ShapeDtypeStruct((steps, pair_rows, hidden_width), F32),
            jax.ShapeDtypeStruct((steps, pair_rows, hidden_width), F32),
            jax.ShapeDtypeStruct((steps, pair_rows, hidden_width), BF16),
        ]
        + [jax.ShapeDtypeStruct((steps - 1, block_rows, width), BF16)]
        + [
            jax.ShapeDtypeStruct((2 * hidden_width, width), BF16),
            jax.ShapeDtypeStruct((width, hidden_width), BF16),
        ],
        compiler_params=pltpu.CompilerParams(vmem_limit_bytes=16 << 20),
        cost_estimate=pl.CostEstimate(flops=0, bytes_accessed=0, transcendentals=0),
        name="factors",
    )(
        which,
        pltpu.with_memory_space_constraint(saved[0], pltpu.HBM),
        saved[1],
        pltpu.with_memory_space_constraint(w_in, pltpu.HBM),
        pltpu.with_memory_space_constraint(w_down, pltpu.HBM),
        pltpu.with_memory_space_constraint(fresh_grads, pltpu.HBM),
        fresh_peer,
        payload,
    )

    at_end = section == jnp.where(core == 0, 0, sections - 1)

    blocks, gate_factor, activated = lax.optimization_barrier((blocks, gate_factor, activated))

    def weight_grads(pre_held, dy_all):
        block = lane_block(part_width, 1024)
        blocks_each = part_width // block
        return pl.pallas_call(
            functools.partial(weight_grads_kernel, steps, replicas, tensor_count),
            grid_spec=pltpu.PrefetchScalarGridSpec(
                num_scalar_prefetch=1,
                grid=(2, blocks_each),
                in_specs=[
                    pl.BlockSpec(
                        (1, steps, 1, batch_rows, block),
                        lambda i, j, at: (at[0] ^ i, 0, 0, 0, at[1] * blocks_each + j),
                    )
                ] * replicas
                + [pl.BlockSpec((steps, pair_rows, 3 * hidden_width), lambda i, j, at: (0, 0, 0))] * replicas
                + [pl.BlockSpec((steps * pair_rows, block), lambda i, j, at: (0, at[1] * blocks_each + j))] * replicas,
                out_specs=[
                    pl.BlockSpec((1, 1, block, 2 * hidden_width), lambda i, j, at: (at[0] ^ i, 0, j, 0)),
                    pl.BlockSpec((1, 1, hidden_width, block), lambda i, j, at: (at[0] ^ i, 0, 0, j)),
                ],
                scratch_shapes=[
                    pltpu.VMEM((replicas * steps * batch_rows, 2 * hidden_width), BF16),
                    pltpu.VMEM((replicas * steps * batch_rows, hidden_width), BF16),
                ],
            ),
            out_shape=[
                jax.ShapeDtypeStruct((2, 1, part_width, 2 * hidden_width), F32),
                jax.ShapeDtypeStruct((2, 1, hidden_width, part_width), F32),
            ],
            compiler_params=pltpu.CompilerParams(vmem_limit_bytes=24 << 20),
            cost_estimate=pl.CostEstimate(flops=0, bytes_accessed=0, transcendentals=0),
            name="weight_grads",
        )(
            which,
            *saved,
            *[to_core(pre_held, o) if o else pre_held for o in range(replicas)],
            *dy_all,
        )

    hand_offs = jnp.zeros((2, steps, shard_rows, width), F32)
    hand_rows = steps * pair_rows
    dy_held = jnp.zeros((hand_rows + (steps - 1) * shard_rows, width), BF16)
    pre_held = jnp.zeros((steps, pair_rows, 3 * hidden_width), BF16).at[:, :, 2 * hidden_width:].set(hidden)
    for k in range(steps):
        dy = placed(blocks)
        dy_held = dy_held.at[k * pair_rows:(k + 1) * pair_rows].set(dy)
        if k + 1 == steps:
            dy_all = [to_core(dy_held, o) if o else dy_held for o in range(replicas)]
        dh = jnp.einsum("rd,dh->rh", dy, w_down_dir, preferred_element_type=F32)
        pre_grad = jnp.concatenate([dh * gate_factor[k], dh * activated[k]], axis=1).astype(BF16)
        pre_held = pre_held.at[k, :, :2 * hidden_width].set(pre_grad)
        part = jnp.einsum("rc,cd->rd", pre_grad, w_in_dir, preferred_element_type=F32).astype(BF16)
        part = part.reshape(tensor_count, block_rows, width)

        def part_for(target):
            return lax.dynamic_index_in_dim(part, target, 0, keepdims=False)

        own_part = part_for(place)
        parts = []
        for s in range(1, tensor_count):
            parts.append(rotate(part_for(lax.rem(place + s, tensor_count)), s))
        if k + 1 == steps:
            parts, grads = lax.optimization_barrier((parts, weight_grads(pre_held, dy_all)))
        summed = own_part.astype(F32)
        for x in parts:
            summed = summed + x.astype(F32)
        handed = incoming + summed
        hand_offs = lax.dynamic_update_slice(hand_offs, handed[None, None, :shard_rows], (core, k, 0, 0))
        if k + 1 < steps:
            payload = jnp.where(at_end, fresh_pair[k], handed.astype(BF16))
            blocks = [
                lax.ppermute(payload, AXES, ring_pairs(sections, tensor_count, replicas, s))
                for s in range(tensor_count)
            ]
            leaving = summed if k == 0 else handed
            dy_held = dy_held.at[hand_rows + k * shard_rows:hand_rows + (k + 1) * shard_rows].set(
                leaving[shard_rows:].astype(BF16)
            )
            incoming = blocks[0].astype(F32)
        else:
            last = to_core(handed[shard_rows:])
    for k in range(steps):
        if k + 1 < steps:
            start = hand_rows + k * shard_rows
            arrived = dy_all[1][start:start + shard_rows].astype(F32)
            arrived = arrived + theirs(entry) if k == 0 else arrived
        else:
            arrived = last
        hand_offs = lax.dynamic_update_slice(hand_offs, arrived[None, None], (1 - core, k, 0, 0))
    return (hand_offs[:, :, None], *grads)


def solution(mesh):
    placed = (
        P(None, "pipe", ("dp", "tensor"), None),
        P(None, None, ("dp", "tensor"), None),
        P(None, None, "pipe", "dp", None),
        P(None, "pipe", None, "tensor"),
        P(None, "pipe", "tensor", None),
    )
    return jax.shard_map(
        local,
        mesh=mesh,
        in_specs=placed,
        out_specs=(
            P(None, None, "pipe", ("dp", "tensor"), None),
            P(None, "pipe", "dp", "tensor"),
            P(None, "pipe", "tensor", "dp"),
        ),
        check_vma=False,
    )
```

```python
import functools

import jax
import jax.numpy as jnp
from jax import lax
from jax.experimental import pallas as pl
from jax.experimental.pallas import tpu as pltpu
from jax.sharding import PartitionSpec as P

AXES = ("pipe", "tensor", "dp")
BF16 = jnp.bfloat16
F32 = jnp.float32


def ring_pairs(sections, tensor_count, replicas, shift):
    pairs = []
    for p in range(sections):
        for t in range(tensor_count):
            to = (t + shift) % tensor_count
            for q in range(replicas):
                step = 1 if q % 2 else -1
                if 0 <= p + step < sections:
                    target = ((p + step) * tensor_count + to) * replicas + q
                else:
                    target = (p * tensor_count + to) * replicas + (q ^ 1)
                pairs.append(((p * tensor_count + t) * replicas + q, target))
    return pairs


def lane_block(width, most):
    best = 128
    for size in range(128, most + 1, 128):
        if width % size == 0:
            best = size
    return best


def factors_kernel(
    places, at, own_ref, peer_ref, w_ref, down_ref, fresh_ref, fresh_peer_ref, _,
    gate_ref, up_ref, hidden_ref, fresh_out, w_copy, down_copy, total, mixed
):
    steps, batch_rows, depth = own_ref.shape[1], own_ref.shape[3], own_ref.shape[4]
    shard_rows = batch_rows // places
    hidden_width = hidden_ref.shape[2]
    count = steps * batch_rows
    step = pl.program_id(0)
    rows = jnp.concatenate(
        [own_ref[...].reshape(count, depth), peer_ref[...].reshape(count, depth)], axis=0
    )
    weights = w_ref[0, 0]
    product = jnp.dot(rows, weights, preferred_element_type=F32)
    w_copy[...] = weights.T
    down_copy[...] = down_ref[0, 0].T

    @pl.when(step == 0)
    def _():
        total[...] = product
        for k in range(fresh_out.shape[0]):
            fresh_out[k] = jnp.concatenate(
                [fresh_peer_ref[1 - at[0], k], fresh_ref[1 - at[0], k]], axis=0
            ).astype(BF16)

    @pl.when(step > 0)
    def _():
        total[...] += product

    @pl.when(step == pl.num_programs(0) - 1)
    def _():
        for k in range(steps):
            for j in range(places):
                for r in range(2):
                    source = (r * steps + k) * batch_rows + j * shard_rows
                    target = (2 * j + r) * shard_rows
                    mixed[k, target:target + shard_rows] = total[source:source + shard_rows]
        gate = mixed[:, :, :hidden_width]
        up = mixed[:, :, hidden_width:]
        sigmoid_val = jax.nn.sigmoid(gate)
        activated = gate * sigmoid_val
        gate_ref[...] = up * sigmoid_val * (1.0 + gate * (1.0 - sigmoid_val))
        up_ref[...] = activated
        hidden_ref[...] = (activated * up).astype(BF16)


def weight_grads_kernel(steps, replicas, places, _, *refs):
    saved, pre, dy = refs[:replicas], refs[replicas:2 * replicas], refs[2 * replicas:3 * replicas]
    pair_rows = 2 * saved[0].shape[3]
    in_ref, down_ref, pre_rows, hidden_rows = refs[-4:]
    batch_rows, block = saved[0].shape[3], saved[0].shape[4]
    shard_rows = batch_rows // places
    hidden_width = hidden_rows.shape[1]
    count = steps * batch_rows

    for parity in range(2):

        @pl.when(pl.program_id(0) == parity)
        def _(parity=parity):
            @pl.when(pl.program_id(1) == 0)
            def _():
                for pair in range(replicas // 2):
                    held = pre[2 * pair + parity]
                    hidden_rows[pair * 2 * count:(pair + 1) * 2 * count] = held[:, 2 * hidden_width:3 * hidden_width]
                    for k in range(steps):
                        values = held[k * pair_rows:(k + 1) * pair_rows, :2 * hidden_width].astype(F32)
                        for r in range(2):
                            half = jnp.concatenate(
                                [
                                    values[(2 * j + r) * shard_rows:(2 * j + r + 1) * shard_rows]
                                    for j in range(places)
                                ],
                                axis=0,
                            )
                            start = ((2 * pair + (r ^ parity)) * steps + k) * batch_rows
                            pre_rows[start:start + batch_rows] = half.astype(BF16)

            down_ref[0, 0] = lax.dot_general(
                hidden_rows[...],
                jnp.concatenate([dy[offset][...] for offset in range(parity, replicas, 2)], axis=0),
                (((0,), (0,)), ((), ())),
                preferred_element_type=F32,
            )

    inputs = jnp.concatenate([x[...].reshape(count, block) for x in saved], axis=0)
    in_ref[0, 0] = lax.dot_general(
        inputs, pre_rows[...], (((0,), (0,)), ((), ())), preferred_element_type=F32
    )


def local(entry_grads, fresh_grads, saved_inputs, w_in, w_down):
    section = lax.axis_index("pipe")
    sections = lax.axis_size("pipe")
    place = lax.axis_index("tensor")
    tensor_count = lax.axis_size("tensor")
    replica = lax.axis_index("dp")
    replicas = lax.axis_size("dp")
    core = lax.rem(replica, 2)
    steps, _, batch_rows, width = saved_inputs.shape[1:]
    shard_rows = batch_rows // tensor_count
    block_rows = 2 * shard_rows
    pair_rows = 2 * batch_rows
    hidden_width = w_down.shape[2]
    part_width = width // replicas

    def mine(x):
        return jnp.where(core == 0, x[0], x[1])

    def theirs(x):
        return jnp.where(core == 0, x[1], x[0])

    def indexed(x):
        return lax.dynamic_index_in_dim(x, core, 0, keepdims=False)

    def by_direction(own, other):
        return jnp.where(core == 0, jnp.stack([own, other]), jnp.stack([other, own]))

    def to_core(x, offset=1):
        return lax.ppermute(x, "dp", [(i, i ^ offset) for i in range(replicas)])

    def rotate(x, shift):
        return lax.ppermute(x, "tensor", [(i, (i + shift) % tensor_count) for i in range(tensor_count)])

    def placed(blocks):
        rows = []
        for source in range(tensor_count):
            shift = lax.rem(place - source + tensor_count, tensor_count)
            block = blocks[0]
            for i in range(1, tensor_count):
                block = jnp.where(shift == i, blocks[i], block)
            rows.append(block)
        return jnp.concatenate(rows)

    entry = entry_grads[:, 0]
    entry_peer = to_core(entry_grads)[:, 0]
    fresh_peer = to_core(fresh_grads)
    incoming = jnp.concatenate([mine(entry), mine(entry_peer)])
    payload = incoming.astype(BF16)
    blocks = [payload] + [rotate(payload, s) for s in range(1, tensor_count)]
    saved = [saved_inputs] + [to_core(saved_inputs, offset) for offset in range(1, replicas)]
    which = jnp.stack([core, replica]).astype(jnp.int32)
    depth = lane_block(width, 1792)
    gate_factor, activated, hidden, fresh_pair, w_in_dir, w_down_dir = pl.pallas_call(
        functools.partial(factors_kernel, tensor_count),
        grid_spec=pltpu.PrefetchScalarGridSpec(
            num_scalar_prefetch=1,
            grid=(width // depth,),
            in_specs=[
                pl.BlockSpec((1, steps, 1, batch_rows, depth), lambda i, at: (at[0], 0, 0, 0, i)),
                pl.BlockSpec((1, steps, 1, batch_rows, depth), lambda i, at: (at[0], 0, 0, 0, i)),
                pl.BlockSpec((1, 1, depth, 2 * hidden_width), lambda i, at: (at[0], 0, i, 0)),
                pl.BlockSpec((1, 1, hidden_width, depth), lambda i, at: (at[0], 0, 0, i)),
                pl.BlockSpec(fresh_grads.shape, lambda i, at: (0, 0, 0, 0)),
                pl.BlockSpec(fresh_grads.shape, lambda i, at: (0, 0, 0, 0)),
                pl.BlockSpec(memory_space=pl.ANY),
            ],
            out_specs=[pl.BlockSpec((steps, pair_rows, hidden_width), lambda i, at: (0, 0, 0))] * 3
            + [pl.BlockSpec((steps - 1, block_rows, width), lambda i, at: (0, 0, 0))]
            + [
                pl.BlockSpec((2 * hidden_width, depth), lambda i, at: (0, i)),
                pl.BlockSpec((depth, hidden_width), lambda i, at: (i, 0)),
            ],
            scratch_shapes=[
                pltpu.VMEM((2 * steps * batch_rows, 2 * hidden_width), F32),
                pltpu.VMEM((steps, pair_rows, 2 * hidden_width), F32),
            ],
        ),
        out_shape=[
            jax.ShapeDtypeStruct((steps, pair_rows, hidden_width), F32),
            jax.ShapeDtypeStruct((steps, pair_rows, hidden_width), F32),
            jax.ShapeDtypeStruct((steps, pair_rows, hidden_width), BF16),
        ]
        + [jax.ShapeDtypeStruct((steps - 1, block_rows, width), BF16)]
        + [
            jax.ShapeDtypeStruct((2 * hidden_width, width), BF16),
            jax.ShapeDtypeStruct((width, hidden_width), BF16),
        ],
        compiler_params=pltpu.CompilerParams(vmem_limit_bytes=16 << 20),
        cost_estimate=pl.CostEstimate(flops=0, bytes_accessed=0, transcendentals=0),
        name="factors",
    )(
        which,
        pltpu.with_memory_space_constraint(saved[0], pltpu.HBM),
        saved[1],
        pltpu.with_memory_space_constraint(w_in, pltpu.HBM),
        pltpu.with_memory_space_constraint(w_down, pltpu.HBM),
        pltpu.with_memory_space_constraint(fresh_grads, pltpu.HBM),
        fresh_peer,
        payload,
    )

    at_end = section == jnp.where(core == 0, 0, sections - 1)

    blocks, gate_factor, activated = lax.optimization_barrier((blocks, gate_factor, activated))

    block = lane_block(part_width, 1024)
    blocks_each = part_width // block
    dy_start = -(-3 * hidden_width // block) * block

    def weight_grads(held_all):
        return pl.pallas_call(
            functools.partial(weight_grads_kernel, steps, replicas, tensor_count),
            grid_spec=pltpu.PrefetchScalarGridSpec(
                num_scalar_prefetch=1,
                grid=(2, blocks_each),
                in_specs=[
                    pl.BlockSpec(
                        (1, steps, 1, batch_rows, block),
                        lambda i, j, at: (at[0] ^ i, 0, 0, 0, at[1] * blocks_each + j),
                    )
                ] * replicas
                + [pl.BlockSpec((steps * pair_rows, dy_start), lambda i, j, at: (0, 0))] * replicas
                + [
                    pl.BlockSpec(
                        (steps * pair_rows, block),
                        lambda i, j, at: (0, dy_start // block + at[1] * blocks_each + j),
                    )
                ]
                * replicas,
                out_specs=[
                    pl.BlockSpec((1, 1, block, 2 * hidden_width), lambda i, j, at: (at[0] ^ i, 0, j, 0)),
                    pl.BlockSpec((1, 1, hidden_width, block), lambda i, j, at: (at[0] ^ i, 0, 0, j)),
                ],
                scratch_shapes=[
                    pltpu.VMEM((replicas * steps * batch_rows, 2 * hidden_width), BF16),
                    pltpu.VMEM((replicas * steps * batch_rows, hidden_width), BF16),
                ],
            ),
            out_shape=[
                jax.ShapeDtypeStruct((2, 1, part_width, 2 * hidden_width), F32),
                jax.ShapeDtypeStruct((2, 1, hidden_width, part_width), F32),
            ],
            compiler_params=pltpu.CompilerParams(vmem_limit_bytes=24 << 20),
            cost_estimate=pl.CostEstimate(flops=0, bytes_accessed=0, transcendentals=0),
            name="weight_grads",
        )(
            which,
            *saved,
            *held_all,
            *held_all,
        )

    hand_offs = jnp.zeros((2, steps, shard_rows, width), F32)
    hand_rows = steps * pair_rows
    held = jnp.zeros((hand_rows + (steps - 1) * shard_rows, dy_start + width), BF16)
    held = lax.dynamic_update_slice(held, hidden.reshape(hand_rows, hidden_width), (0, 2 * hidden_width))
    for k in range(steps):
        dy = placed(blocks)
        held = lax.dynamic_update_slice(held, dy, (k * pair_rows, dy_start))
        dh = jnp.einsum("rd,dh->rh", dy, w_down_dir, preferred_element_type=F32)
        pre_grad = jnp.concatenate([dh * gate_factor[k], dh * activated[k]], axis=1).astype(BF16)
        held = lax.dynamic_update_slice(held, pre_grad, (k * pair_rows, 0))
        if k + 1 == steps:
            held_all = [to_core(held, o) if o else held for o in range(replicas)]
        part = jnp.einsum("rc,cd->rd", pre_grad, w_in_dir, preferred_element_type=F32).astype(BF16)
        part = part.reshape(tensor_count, block_rows, width)

        def part_for(target):
            return lax.dynamic_index_in_dim(part, target, 0, keepdims=False)

        own_part = part_for(place)
        parts = []
        for s in [*range(1, tensor_count, 2), *range(2, tensor_count, 2)]:
            parts.append(rotate(part_for(lax.rem(place + s, tensor_count)), s))
        if k + 1 == steps:
            parts, grads = lax.optimization_barrier((parts, weight_grads(held_all)))
        summed = own_part.astype(F32)
        for x in parts:
            summed = summed + x.astype(F32)
        handed = incoming + summed
        hand_offs = lax.dynamic_update_slice(hand_offs, handed[None, None, :shard_rows], (core, k, 0, 0))
        if k + 1 < steps:
            payload = jnp.where(at_end, fresh_pair[k], handed.astype(BF16))
            blocks = [
                lax.ppermute(payload, AXES, ring_pairs(sections, tensor_count, replicas, s))
                for s in range(tensor_count)
            ]
            leaving = summed if k == 0 else handed
            held = lax.dynamic_update_slice(
                held, leaving[shard_rows:].astype(BF16), (hand_rows + k * shard_rows, dy_start)
            )
            incoming = blocks[0].astype(F32)
        else:
            last = to_core(handed[shard_rows:])
    for k in range(steps):
        if k + 1 < steps:
            start = hand_rows + k * shard_rows
            arrived = held_all[1][start:start + shard_rows, dy_start:].astype(F32)
            arrived = arrived + theirs(entry) if k == 0 else arrived
        else:
            arrived = last
        hand_offs = lax.dynamic_update_slice(hand_offs, arrived[None, None], (1 - core, k, 0, 0))
    return (hand_offs[:, :, None], *grads)


def solution(mesh):
    placed = (
        P(None, "pipe", ("dp", "tensor"), None),
        P(None, None, ("dp", "tensor"), None),
        P(None, None, "pipe", "dp", None),
        P(None, "pipe", None, "tensor"),
        P(None, "pipe", "tensor", None),
    )
    return jax.shard_map(
        local,
        mesh=mesh,
        in_specs=placed,
        out_specs=(
            P(None, None, "pipe", ("dp", "tensor"), None),
            P(None, "pipe", "dp", "tensor"),
            P(None, "pipe", "tensor", "dp"),
        ),
        check_vma=False,
    )
```

```python
import functools

import jax
import jax.numpy as jnp
from jax import lax
from jax.experimental import pallas as pl
from jax.experimental.pallas import tpu as pltpu
from jax.sharding import PartitionSpec as P

AXES = ("pipe", "tensor", "dp")
BF16 = jnp.bfloat16
F32 = jnp.float32


def ring_pairs(sections, tensor_count, replicas, shift):
    pairs = []
    for p in range(sections):
        for t in range(tensor_count):
            to = (t + shift) % tensor_count
            for q in range(replicas):
                step = 1 if q % 2 else -1
                if 0 <= p + step < sections:
                    target = ((p + step) * tensor_count + to) * replicas + q
                else:
                    target = (p * tensor_count + to) * replicas + (q ^ 1)
                pairs.append(((p * tensor_count + t) * replicas + q, target))
    return pairs


def lane_block(width, most):
    best = 128
    for size in range(128, most + 1, 128):
        if width % size == 0:
            best = size
    return best


def factors_kernel(
    places, at, own_ref, peer_ref, w_ref, down_ref, fresh_ref, fresh_peer_ref, _,
    gate_ref, up_ref, hidden_ref, fresh_out, w_copy, down_copy, total, mixed
):
    steps, batch_rows, depth = own_ref.shape[1], own_ref.shape[3], own_ref.shape[4]
    shard_rows = batch_rows // places
    hidden_width = hidden_ref.shape[2]
    count = steps * batch_rows
    step = pl.program_id(0)
    rows = jnp.concatenate(
        [own_ref[...].reshape(count, depth), peer_ref[...].reshape(count, depth)], axis=0
    )
    weights = w_ref[0, 0]
    product = jnp.dot(rows, weights, preferred_element_type=F32)
    w_copy[...] = weights.T
    down_copy[...] = down_ref[0, 0].T

    @pl.when(step == 0)
    def _():
        total[...] = product
        for k in range(fresh_out.shape[0]):
            fresh_out[k] = jnp.concatenate(
                [fresh_peer_ref[1 - at[0], k], fresh_ref[1 - at[0], k]], axis=0
            ).astype(BF16)

    @pl.when(step > 0)
    def _():
        total[...] += product

    @pl.when(step == pl.num_programs(0) - 1)
    def _():
        for k in range(steps):
            for j in range(places):
                for r in range(2):
                    source = (r * steps + k) * batch_rows + j * shard_rows
                    target = (2 * j + r) * shard_rows
                    mixed[k, target:target + shard_rows] = total[source:source + shard_rows]
        gate = mixed[:, :, :hidden_width]
        up = mixed[:, :, hidden_width:]
        sigmoid_val = jax.nn.sigmoid(gate)
        activated = gate * sigmoid_val
        gate_ref[...] = up * sigmoid_val * (1.0 + gate * (1.0 - sigmoid_val))
        up_ref[...] = activated
        hidden_ref[...] = (activated * up).astype(BF16)


def weight_grads_kernel(steps, replicas, places, _, *refs):
    saved, pre, dy = refs[:replicas], refs[replicas:2 * replicas], refs[2 * replicas:3 * replicas]
    pair_rows = 2 * saved[0].shape[3]
    in_ref, down_ref, pre_rows, hidden_rows = refs[-4:]
    batch_rows, block = saved[0].shape[3], saved[0].shape[4]
    shard_rows = batch_rows // places
    hidden_width = hidden_rows.shape[1]
    count = steps * batch_rows

    for parity in range(2):

        @pl.when(pl.program_id(0) == parity)
        def _(parity=parity):
            @pl.when(pl.program_id(1) == 0)
            def _():
                for pair in range(replicas // 2):
                    held = pre[2 * pair + parity]
                    hidden_rows[pair * 2 * count:(pair + 1) * 2 * count] = held[:, 2 * hidden_width:3 * hidden_width]
                    for k in range(steps):
                        values = held[k * pair_rows:(k + 1) * pair_rows, :2 * hidden_width].astype(F32)
                        for r in range(2):
                            half = jnp.concatenate(
                                [
                                    values[(2 * j + r) * shard_rows:(2 * j + r + 1) * shard_rows]
                                    for j in range(places)
                                ],
                                axis=0,
                            )
                            start = ((2 * pair + (r ^ parity)) * steps + k) * batch_rows
                            pre_rows[start:start + batch_rows] = half.astype(BF16)

            down_ref[0, 0] = lax.dot_general(
                hidden_rows[...],
                jnp.concatenate([dy[offset][...] for offset in range(parity, replicas, 2)], axis=0),
                (((0,), (0,)), ((), ())),
                preferred_element_type=F32,
            )

    inputs = jnp.concatenate([x[...].reshape(count, block) for x in saved], axis=0)
    in_ref[0, 0] = lax.dot_general(
        inputs, pre_rows[...], (((0,), (0,)), ((), ())), preferred_element_type=F32
    )


def local(entry_grads, fresh_grads, saved_inputs, w_in, w_down):
    section = lax.axis_index("pipe")
    sections = lax.axis_size("pipe")
    place = lax.axis_index("tensor")
    tensor_count = lax.axis_size("tensor")
    replica = lax.axis_index("dp")
    replicas = lax.axis_size("dp")
    core = lax.rem(replica, 2)
    steps, _, batch_rows, width = saved_inputs.shape[1:]
    shard_rows = batch_rows // tensor_count
    block_rows = 2 * shard_rows
    pair_rows = 2 * batch_rows
    hidden_width = w_down.shape[2]
    part_width = width // replicas

    def mine(x):
        return jnp.where(core == 0, x[0], x[1])

    def theirs(x):
        return jnp.where(core == 0, x[1], x[0])

    def indexed(x):
        return lax.dynamic_index_in_dim(x, core, 0, keepdims=False)

    def by_direction(own, other):
        return jnp.where(core == 0, jnp.stack([own, other]), jnp.stack([other, own]))

    def to_core(x, offset=1):
        return lax.ppermute(x, "dp", [(i, i ^ offset) for i in range(replicas)])

    def rotate(x, shift):
        return lax.ppermute(x, "tensor", [(i, (i + shift) % tensor_count) for i in range(tensor_count)])

    def placed(blocks):
        rows = []
        for source in range(tensor_count):
            shift = lax.rem(place - source + tensor_count, tensor_count)
            block = blocks[0]
            for i in range(1, tensor_count):
                block = jnp.where(shift == i, blocks[i], block)
            rows.append(block)
        return jnp.concatenate(rows)

    entry = entry_grads[:, 0]
    entry_peer = to_core(entry_grads)[:, 0]
    fresh_peer = to_core(fresh_grads)
    incoming = jnp.concatenate([mine(entry), mine(entry_peer)])
    payload = incoming.astype(BF16)
    blocks = [payload] + [rotate(payload, s) for s in range(1, tensor_count)]
    saved = [saved_inputs] + [to_core(saved_inputs, offset) for offset in range(1, replicas)]
    which = jnp.stack([core, replica]).astype(jnp.int32)
    depth = lane_block(width, 1792)
    gate_factor, activated, hidden, fresh_pair, w_in_dir, w_down_dir = pl.pallas_call(
        functools.partial(factors_kernel, tensor_count),
        grid_spec=pltpu.PrefetchScalarGridSpec(
            num_scalar_prefetch=1,
            grid=(width // depth,),
            in_specs=[
                pl.BlockSpec((1, steps, 1, batch_rows, depth), lambda i, at: (at[0], 0, 0, 0, i)),
                pl.BlockSpec((1, steps, 1, batch_rows, depth), lambda i, at: (at[0], 0, 0, 0, i)),
                pl.BlockSpec((1, 1, depth, 2 * hidden_width), lambda i, at: (at[0], 0, i, 0)),
                pl.BlockSpec((1, 1, hidden_width, depth), lambda i, at: (at[0], 0, 0, i)),
                pl.BlockSpec(fresh_grads.shape, lambda i, at: (0, 0, 0, 0)),
                pl.BlockSpec(fresh_grads.shape, lambda i, at: (0, 0, 0, 0)),
                pl.BlockSpec(memory_space=pl.ANY),
            ],
            out_specs=[pl.BlockSpec((steps, pair_rows, hidden_width), lambda i, at: (0, 0, 0))] * 3
            + [pl.BlockSpec((steps - 1, block_rows, width), lambda i, at: (0, 0, 0))]
            + [
                pl.BlockSpec((2 * hidden_width, depth), lambda i, at: (0, i)),
                pl.BlockSpec((depth, hidden_width), lambda i, at: (i, 0)),
            ],
            scratch_shapes=[
                pltpu.VMEM((2 * steps * batch_rows, 2 * hidden_width), F32),
                pltpu.VMEM((steps, pair_rows, 2 * hidden_width), F32),
            ],
        ),
        out_shape=[
            jax.ShapeDtypeStruct((steps, pair_rows, hidden_width), F32),
            jax.ShapeDtypeStruct((steps, pair_rows, hidden_width), F32),
            jax.ShapeDtypeStruct((steps, pair_rows, hidden_width), BF16),
        ]
        + [jax.ShapeDtypeStruct((steps - 1, block_rows, width), BF16)]
        + [
            jax.ShapeDtypeStruct((2 * hidden_width, width), BF16),
            jax.ShapeDtypeStruct((width, hidden_width), BF16),
        ],
        compiler_params=pltpu.CompilerParams(vmem_limit_bytes=16 << 20),
        cost_estimate=pl.CostEstimate(flops=0, bytes_accessed=0, transcendentals=0),
        name="factors",
    )(
        which,
        pltpu.with_memory_space_constraint(saved[0], pltpu.HBM),
        saved[1],
        pltpu.with_memory_space_constraint(w_in, pltpu.HBM),
        pltpu.with_memory_space_constraint(w_down, pltpu.HBM),
        pltpu.with_memory_space_constraint(fresh_grads, pltpu.HBM),
        fresh_peer,
        payload,
    )

    at_end = section == jnp.where(core == 0, 0, sections - 1)

    blocks, gate_factor, activated = lax.optimization_barrier((blocks, gate_factor, activated))

    block = lane_block(part_width, 1024)
    blocks_each = part_width // block
    dy_start = -(-3 * hidden_width // block) * block

    def weight_grads(held_all):
        return pl.pallas_call(
            functools.partial(weight_grads_kernel, steps, replicas, tensor_count),
            grid_spec=pltpu.PrefetchScalarGridSpec(
                num_scalar_prefetch=1,
                grid=(2, blocks_each),
                in_specs=[
                    pl.BlockSpec(
                        (1, steps, 1, batch_rows, block),
                        lambda i, j, at: (at[0] ^ i, 0, 0, 0, at[1] * blocks_each + j),
                    )
                ] * replicas
                + [pl.BlockSpec((steps * pair_rows, dy_start), lambda i, j, at: (0, 0))] * replicas
                + [
                    pl.BlockSpec(
                        (steps * pair_rows, block),
                        lambda i, j, at: (0, dy_start // block + at[1] * blocks_each + j),
                    )
                ]
                * replicas,
                out_specs=[
                    pl.BlockSpec((1, 1, block, 2 * hidden_width), lambda i, j, at: (at[0] ^ i, 0, j, 0)),
                    pl.BlockSpec((1, 1, hidden_width, block), lambda i, j, at: (at[0] ^ i, 0, 0, j)),
                ],
                scratch_shapes=[
                    pltpu.VMEM((replicas * steps * batch_rows, 2 * hidden_width), BF16),
                    pltpu.VMEM((replicas * steps * batch_rows, hidden_width), BF16),
                ],
            ),
            out_shape=[
                jax.ShapeDtypeStruct((2, 1, part_width, 2 * hidden_width), F32),
                jax.ShapeDtypeStruct((2, 1, hidden_width, part_width), F32),
            ],
            compiler_params=pltpu.CompilerParams(vmem_limit_bytes=24 << 20),
            cost_estimate=pl.CostEstimate(flops=0, bytes_accessed=0, transcendentals=0),
            name="weight_grads",
        )(
            which,
            *saved,
            *held_all,
            *held_all,
        )

    hand_offs = jnp.zeros((2, steps, shard_rows, width), F32)
    hand_rows = steps * pair_rows
    held = jnp.zeros((hand_rows + (steps - 1) * shard_rows, dy_start + width), BF16)
    held = lax.dynamic_update_slice(held, hidden.reshape(hand_rows, hidden_width), (0, 2 * hidden_width))
    for k in range(steps):
        dy = placed(blocks)
        held = lax.dynamic_update_slice(held, dy, (k * pair_rows, dy_start))
        dh = jnp.einsum("rd,dh->rh", dy, w_down_dir, preferred_element_type=F32)
        pre_grad = jnp.concatenate([dh * gate_factor[k], dh * activated[k]], axis=1).astype(BF16)
        held = lax.dynamic_update_slice(held, pre_grad, (k * pair_rows, 0))
        if k + 1 == steps:
            held_all = [to_core(held, o) if o else held for o in range(replicas)]
        part = jnp.einsum("rc,cd->rd", pre_grad, w_in_dir, preferred_element_type=F32).astype(BF16)
        part = part.reshape(tensor_count, block_rows, width)

        def part_for(target):
            return lax.dynamic_index_in_dim(part, target, 0, keepdims=False)

        own_part = part_for(place)
        parts = []
        for s in range(1, tensor_count) if k + 1 == steps else [*range(1, tensor_count, 2), *range(2, tensor_count, 2)]:
            parts.append(rotate(part_for(lax.rem(place + s, tensor_count)), s))
        if k + 1 == steps:
            parts, grads = lax.optimization_barrier((parts, weight_grads(held_all)))
        summed = own_part.astype(F32)
        for x in parts:
            summed = summed + x.astype(F32)
        handed = incoming + summed
        hand_offs = lax.dynamic_update_slice(hand_offs, handed[None, None, :shard_rows], (core, k, 0, 0))
        if k + 1 < steps:
            payload = jnp.where(at_end, fresh_pair[k], handed.astype(BF16))
            blocks = [
                lax.ppermute(payload, AXES, ring_pairs(sections, tensor_count, replicas, s))
                for s in range(tensor_count)
            ]
            leaving = summed if k == 0 else handed
            held = lax.dynamic_update_slice(
                held, leaving[shard_rows:].astype(BF16), (hand_rows + k * shard_rows, dy_start)
            )
            incoming = blocks[0].astype(F32)
        else:
            last = to_core(handed[shard_rows:])
    for k in range(steps):
        if k + 1 < steps:
            start = hand_rows + k * shard_rows
            arrived = held_all[1][start:start + shard_rows, dy_start:].astype(F32)
            arrived = arrived + theirs(entry) if k == 0 else arrived
        else:
            arrived = last
        hand_offs = lax.dynamic_update_slice(hand_offs, arrived[None, None], (1 - core, k, 0, 0))
    return (hand_offs[:, :, None], *grads)


def solution(mesh):
    placed = (
        P(None, "pipe", ("dp", "tensor"), None),
        P(None, None, ("dp", "tensor"), None),
        P(None, None, "pipe", "dp", None),
        P(None, "pipe", None, "tensor"),
        P(None, "pipe", "tensor", None),
    )
    return jax.shard_map(
        local,
        mesh=mesh,
        in_specs=placed,
        out_specs=(
            P(None, None, "pipe", ("dp", "tensor"), None),
            P(None, "pipe", "dp", "tensor"),
            P(None, "pipe", "tensor", "dp"),
        ),
        check_vma=False,
    )
```
